32 devices in a mesh: grp: 4 (over y, x), fsdp: 4 (over z), tp: 2 (over core).
Axes of the slice: x: 2, y: 2, z: 4, core: 2. Of those that a mesh axis runs over, the one named last changes fastest.
Arguments:
- image_rows: bfloat16 [6144, 8192], P(('grp', 'fsdp'), 'tp'), may hold values from -6 to 6
- enc_gain: bfloat16 [8192], P('tp'), may hold values from 0.099609375 to 1.8984375
- key_value_w: bfloat16 [8192, 1024], P(('tp', 'fsdp')), may hold values from -0.0625 to 0.0625
- tiles: int32 [24], P('fsdp'), may hold values from 1 to 4
- queries: bfloat16 [4096, 4096], P(('grp', 'fsdp'), 'tp'), may hold values from -6 to 6
Outputs:
- attended: bfloat16 [4096, 4096], P(('grp', 'fsdp'), 'tp')
The draws below stay inside these ranges and needn't reach their ends.
Inputs may be any that keep to these rules, and one draw needn't show every extreme that they name: Each sample has 1 to 4 tiles.
All inputs are finite; a program needn't handle non-finite values.
Results may differ from the reference program's by a relative error of at most 0.0077.
Values may be sent and summed in bfloat16 or wider, within the bound.
No kernel may reach another device: no remote copies, remote signals or barrier semaphores. Data moves between devices by JAX's collectives and lax.ppermute only.
A program may use at most 64 MiB of HBM per device.

```python
import jax
import jax.numpy as jnp
from jax import lax

D = 8192
HD = 128
KVH = 4
QH = 32
TILE_TOK = 16
SAMP = 2
TXT_S = 128
CAP = 64
IMG = 128
TXT = 256
N_GRP = 4
N_FSDP = 4


def touch_ends(entries, stream_key, smallest, top_value):
    shape = entries.shape
    index_at = [jax.random.randint(jax.random.fold_in(stream_key, axis), (), 0, shape[axis]) for axis in range(len(shape))]
    entries = entries.at[tuple(index_at)].set(smallest)
    longest = shape.index(max(shape))
    index_at[longest] = (index_at[longest] + 1) % shape[longest]
    return entries.at[tuple(index_at)].set(top_value)


def block_levels(rng, dims, cuts, smallest, top_value):
    def one(axis_at, parts):
        steps = jax.random.uniform(jax.random.fold_in(jax.random.fold_in(rng, 6), axis_at), (parts,), jnp.float32, smallest / len(cuts), top_value / len(cuts))
        return jnp.repeat(jnp.exp(steps), dims[axis_at] // parts).reshape((-1,) + (1,) * (len(dims) - axis_at - 1))

    level = one(*cuts[0])
    for cut in cuts[1:]:
        level = level * one(*cut)
    return level


def gaussian(stream_key, shape, spread, most, split=(), held_as=jnp.bfloat16):
    loudness = block_levels(stream_key, shape, split, -0.22, 0.18) if split else 1.0
    result = jax.random.normal(stream_key, shape, jnp.float32) * spread * loudness
    return jnp.minimum(jnp.maximum(result, -most), most).astype(held_as)


def setup_inputs(seed: int = 0) -> dict:
    key_list = jax.random.split(jax.random.key(seed), 6)
    return {
        "image_rows": gaussian(key_list[0], (N_GRP * N_FSDP * 3 * IMG, D), 1.0, 6.0, ((0, 16), (1, 2))),
        "enc_gain": jnp.clip(1.0 + 0.18 * jax.random.normal(key_list[1], (D,), jnp.float32), 0.099609375, 1.8984375).astype(jnp.bfloat16),
        "key_value_w": gaussian(key_list[2], (D, KVH * 2 * HD), D ** -0.5, 0.0625, ((0, 8),)),
        "tiles": touch_ends(jax.random.randint(key_list[3], (N_FSDP * 3 * SAMP,), 1, 5), jax.random.fold_in(key_list[3], 1), 1, 4).astype(jnp.int32),
        "queries": gaussian(key_list[4], (N_GRP * N_FSDP * TXT, QH * HD), 1.0, 6.0, ((0, 16), (1, 2))),
    }


def reference(image_rows, enc_gain, key_value_w, tiles, queries):
    rows = image_rows[:N_FSDP * 3 * IMG].astype(jnp.float32)
    mean_sq = lax.optimization_barrier(jnp.mean(rows * rows, axis=1, keepdims=True))
    normed = (rows * lax.rsqrt(mean_sq + 1e-05) * enc_gain.astype(jnp.float32)).astype(jnp.bfloat16)
    kv = jnp.dot(normed, key_value_w, preferred_element_type=jnp.float32).astype(jnp.bfloat16)
    kv = kv.reshape(N_FSDP, 3, SAMP, CAP, KVH, 2, HD)
    keys = jnp.swapaxes(kv[..., 0, :], 0, 1)
    values = jnp.swapaxes(kv[..., 1, :], 0, 1)
    query = queries.reshape(N_GRP, N_FSDP, SAMP, TXT_S, KVH, QH // KVH, HD)
    counts = tiles.reshape(N_FSDP, 3, SAMP) * TILE_TOK
    valid = jnp.arange(CAP)[None, None, None, :] < counts[..., None]
    valid = jnp.swapaxes(valid, 0, 1)
    scale = 1.0 / HD ** 0.5

    def one_group(items):
        q_part, k_part, v_part, live = items
        scores = jnp.einsum('fsikgd,fsjkd->fskgij', q_part.astype(jnp.float32), k_part.astype(jnp.float32)) * scale
        scores = jnp.where(live[:, :, None, None, None, :], scores, -1e+30)
        top = lax.optimization_barrier(jnp.max(scores, axis=-1, keepdims=True))
        expo = jnp.exp(scores - top)
        weights = (expo / lax.optimization_barrier(jnp.sum(expo, axis=-1, keepdims=True))).astype(jnp.bfloat16)
        out = jnp.einsum('fskgij,fsjkd->fsikgd', weights.astype(jnp.float32), v_part.astype(jnp.float32))
        return out.astype(jnp.bfloat16)
    outs = lax.map(one_group, (query[1:], keys, values, valid))
    zero_block = jnp.zeros((1,) + outs.shape[1:], jnp.bfloat16)
    full = jnp.concatenate([zero_block, outs], axis=0)
    return full.reshape(N_GRP * N_FSDP * TXT, QH * HD)
```

```python
import jax
import jax.numpy as jnp
from jax import lax
from jax.sharding import PartitionSpec as P

D = 8192
HD = 128
KVH = 4
QH = 32
TILE_TOK = 16
SAMP = 2
TXT_S = 128
CAP = 64
AXES = ("grp", "fsdp", "tp")


def normed_rows(image_rows, enc_gain, sum_cores):
    rows = image_rows.astype(jnp.float32)
    squares = sum_cores(jnp.sum(rows * rows, axis=1, keepdims=True))
    return (rows * lax.rsqrt(squares / D + 1e-05) * enc_gain.astype(jnp.float32)).astype(
        jnp.bfloat16
    )


def attend(kv, tiles, queries, group):
    local_kv = kv.shape[1]
    groups_q = QH // KVH
    kv = kv.reshape(SAMP, CAP, local_kv, 2 * HD)
    keys = kv[..., :HD]
    values = kv[..., HD:]
    query = queries.reshape(SAMP, TXT_S, local_kv, groups_q, HD)
    counts = lax.dynamic_slice_in_dim(tiles, jnp.maximum(group - 1, 0) * SAMP, SAMP) * TILE_TOK
    live = jnp.arange(CAP)[None, :] < counts[:, None]
    scores = jnp.einsum("sikgd,sjkd->skgij", query, keys, preferred_element_type=jnp.float32) * (
        1.0 / HD**0.5
    )
    scores = jnp.where(live[:, None, None, None, :], scores, -1e30)
    top = jnp.max(scores, axis=-1, keepdims=True)
    expo = jnp.exp(scores - top)
    weights = (expo / jnp.sum(expo, axis=-1, keepdims=True)).astype(jnp.bfloat16)
    out = jnp.einsum(
        "skgij,sjkd->sikgd", weights, values, preferred_element_type=jnp.float32
    ).astype(jnp.bfloat16)
    out = jnp.where(group > 0, out, jnp.zeros_like(out))
    return out.reshape(queries.shape[0], queries.shape[1])


def shards_any(image_rows, enc_gain, key_value_w, tiles, queries):
    group = lax.axis_index("grp")
    per_group = image_rows.shape[0] // 3
    heads_kv = key_value_w.shape[1] // (2 * HD)
    normed = normed_rows(image_rows, enc_gain, lambda s: lax.psum(s, "tp"))
    parts = normed.reshape((3, per_group, normed.shape[1]))
    slots = jnp.concatenate([jnp.zeros_like(parts[:1]), parts], axis=0)
    mine = lax.all_to_all(slots, "grp", split_axis=0, concat_axis=0, tiled=True)[0]
    total = jnp.dot(
        mine,
        lax.all_gather(key_value_w, "fsdp", axis=0, tiled=True),
        preferred_element_type=jnp.float32,
    )
    heads = lax.psum_scatter(
        total.reshape(per_group, heads_kv, 2 * HD), "tp", scatter_dimension=1, tiled=True
    )
    return attend(heads.astype(jnp.bfloat16), tiles, queries, group)


def shards_line(image_rows, enc_gain, key_value_w, tiles, queries):
    g, f, t = (lax.axis_index(a) for a in AXES)
    n_rows = image_rows.shape[0]
    per_group = n_rows // 3
    width = key_value_w.shape[1]
    half = width // 2
    depth = key_value_w.shape[0]
    quarter = depth // 4

    def send(x, pairs):
        index = lambda p, c: (p[0] * 4 + p[1]) * 2 + c
        return lax.ppermute(x, AXES, [(index(a, c), index(b, c)) for a, b in pairs for c in (0, 1)])

    def swap(x):
        return lax.ppermute(x, "tp", [(0, 1), (1, 0)])

    own_rows = lax.dynamic_slice_in_dim(key_value_w, g * quarter, quarter, axis=0)
    kept = lax.dynamic_slice_in_dim(own_rows, t * half, half, axis=1)
    given = lax.dynamic_slice_in_dim(own_rows, (1 - t) * half, half, axis=1)
    own = jnp.concatenate([kept, swap(given)], axis=0)
    from_below = send(own, [((c, z), (c, z + 1)) for c in range(4) for z in range(3)])
    from_above = send(own, [((c, z + 1), (c, z)) for c in range(4) for z in range(3)])
    onward = jnp.where((f == 0) | (f == 3), own, jnp.where(f == 2, from_below, from_above))
    from_two = send(
        onward, [((c, a), (c, b)) for c in range(4) for a, b in ((0, 2), (3, 1), (2, 3), (1, 0))]
    )
    from_three = send(from_two, [((c, a), (c, b)) for c in range(4) for a, b in ((2, 3), (1, 0))])

    normed = normed_rows(image_rows, enc_gain, lambda s: s + swap(s))
    pieces = normed.reshape(n_rows, 4, 4, quarter).transpose(2, 1, 0, 3)
    planes = range(4)
    at_d = send(pieces[3, :2], [((0, z), (3, z)) for z in planes])
    at_b = send(pieces[1], [((0, z), (1, z)) for z in planes])
    at_c = send(
        jnp.concatenate([pieces[3, 2:], pieces[2]], axis=0), [((0, z), (2, z)) for z in planes]
    )
    at_d2 = send(at_c[:2], [((2, z), (3, z)) for z in planes])
    mine = jnp.where(
        g == 0,
        pieces[0],
        jnp.where(
            g == 1, at_b, jnp.where(g == 2, at_c[2:], jnp.concatenate([at_d, at_d2], axis=0))
        ),
    )
    rows = jnp.concatenate([mine, swap(mine)], axis=2)

    def part(block, plane):
        return jnp.dot(
            lax.dynamic_index_in_dim(rows, plane, 0, keepdims=False),
            block,
            preferred_element_type=jnp.float32,
        )

    total = (
        part(own, f)
        + part(from_below, jnp.maximum(f - 1, 0))
        + part(from_above, jnp.minimum(f + 1, 3))
        + part(from_two, f ^ 2)
        + part(from_three, 3 - f)
    ).reshape(3, per_group, half)

    def for_group(h):
        return lax.dynamic_index_in_dim(total, jnp.maximum(h - 1, 0), 0, keepdims=False)

    kv = for_group(g)
    for k in (1, 2, 3):
        kv = kv + send(
            for_group(g ^ k).astype(jnp.bfloat16),
            [((a, z), (a ^ k, z)) for a in range(4) if a ^ k for z in planes],
        ).astype(jnp.float32)
    kv = kv.astype(jnp.bfloat16).reshape(per_group, half // (2 * HD), 2 * HD)
    return attend(kv, tiles, queries, g)


def solution(mesh):
    sizes = tuple(mesh.shape[a] for a in AXES)
    return jax.shard_map(
        shards_line if sizes == (4, 4, 2) else shards_any,
        mesh=mesh,
        in_specs=(
            P(("grp", "fsdp"), "tp"),
            P("tp"),
            P(("tp", "fsdp"), None),
            P("fsdp"),
            P(("grp", "fsdp"), "tp"),
        ),
        out_specs=P(("grp", "fsdp"), "tp"),
        check_vma=False,
    )
```

```python
import jax
import jax.numpy as jnp
from jax import lax
from jax.experimental import pallas as pl
from jax.experimental.pallas import tpu as pltpu
from jax.sharding import PartitionSpec as P

D = 8192
HD = 128
KVH = 4
QH = 32
TILE_TOK = 16
SAMP = 2
TXT_S = 128
CAP = 64
AXES = ("grp", "fsdp", "tp")
VMEM = pl.BlockSpec(memory_space=pltpu.VMEM)
SMEM = pl.BlockSpec(memory_space=pltpu.SMEM)
ANY = pl.BlockSpec(memory_space=pl.ANY)
HBM = pl.BlockSpec(memory_space=pltpu.HBM)
LIMIT = 16 * 1024 * 1024
COST = 10


def attend_any(kv, tiles, queries, group):
    local_kv = kv.shape[1]
    groups_q = QH // KVH
    kv = kv.reshape(SAMP, CAP, local_kv, 2 * HD)
    keys = kv[..., :HD]
    values = kv[..., HD:]
    query = queries.reshape(SAMP, TXT_S, local_kv, groups_q, HD)
    counts = lax.dynamic_slice_in_dim(tiles, jnp.maximum(group - 1, 0) * SAMP, SAMP) * TILE_TOK
    live = jnp.arange(CAP)[None, :] < counts[:, None]
    scores = jnp.einsum("sikgd,sjkd->skgij", query, keys, preferred_element_type=jnp.float32) * (
        1.0 / HD**0.5
    )
    scores = jnp.where(live[:, None, None, None, :], scores, -1e30)
    top = jnp.max(scores, axis=-1, keepdims=True)
    expo = jnp.exp(scores - top)
    weights = (expo / jnp.sum(expo, axis=-1, keepdims=True)).astype(jnp.bfloat16)
    out = jnp.einsum(
        "skgij,sjkd->sikgd", weights, values, preferred_element_type=jnp.float32
    ).astype(jnp.bfloat16)
    out = jnp.where(group > 0, out, jnp.zeros_like(out))
    return out.reshape(queries.shape[0], queries.shape[1])


def shards_any(image_rows, enc_gain, key_value_w, tiles, queries):
    group = lax.axis_index("grp")
    per_group = image_rows.shape[0] // 3
    heads_kv = key_value_w.shape[1] // (2 * HD)
    rows = image_rows.astype(jnp.float32)
    squares = lax.psum(jnp.sum(rows * rows, axis=1, keepdims=True), "tp")
    normed = (rows * lax.rsqrt(squares / D + 1e-05) * enc_gain.astype(jnp.float32)).astype(
        jnp.bfloat16
    )
    parts = normed.reshape((3, per_group, normed.shape[1]))
    slots = jnp.concatenate([jnp.zeros_like(parts[:1]), parts], axis=0)
    mine = lax.all_to_all(slots, "grp", split_axis=0, concat_axis=0, tiled=True)[0]
    total = jnp.dot(
        mine,
        lax.all_gather(key_value_w, "fsdp", axis=0, tiled=True),
        preferred_element_type=jnp.float32,
    )
    heads = lax.psum_scatter(
        total.reshape(per_group, heads_kv, 2 * HD), "tp", scatter_dimension=1, tiled=True
    )
    return attend_any(heads.astype(jnp.bfloat16), tiles, queries, group)


def call(body, outs, *args, specs=None, cost=None):
    outs = [jax.ShapeDtypeStruct(s, d) for s, d in outs]
    if cost is not None:
        cost = pl.CostEstimate(flops=cost * 10**9, bytes_accessed=0, transcendentals=0)
    return pl.pallas_call(
        body,
        out_shape=outs,
        in_specs=specs or [SMEM] + [VMEM] * (len(args) - 1),
        out_specs=[VMEM] * len(outs),
        cost_estimate=cost,
        compiler_params=pltpu.CompilerParams(vmem_limit_bytes=LIMIT),
    )(*args)


def join(kept, other, out):
    rows = kept.shape[0]
    out[:rows, :] = kept[...]
    out[rows:, :] = other[...]


def normalise(place, x, squares, other, gain, a, b, c, d_low, d_high):
    width = x.shape[1] // 16

    @pl.when(place[0] == 0)
    def _():
        scale = lax.rsqrt((squares[...] + other[...]) / D + 1e-05)
        for z in range(4):
            for h in range(4):
                cols = slice((z * 4 + h) * width, (z * 4 + h + 1) * width)
                y = x[:, cols].astype(jnp.float32) * scale * gain[:, cols].astype(jnp.float32)
                out, at = ((a, b, c)[h], z) if h < 3 else ((d_low, d_high)[z // 2], z % 2)
                out[at] = y.astype(jnp.bfloat16)


def onward(place, own, below, above, out):
    f = place[1]

    @pl.when((f == 0) | (f == 3))
    def _():
        out[...] = own[...]

    @pl.when(f == 1)
    def _():
        out[...] = above[...]

    @pl.when(f == 2)
    def _():
        out[...] = below[...]


def later(x, after, out):
    del after
    out[...] = x[...]


def landed(place, a, b, c, d_low, d_high, low, high):
    g = place[0]
    for who, source in ((0, a), (1, b), (2, c)):

        @pl.when(g == who)
        def _(source=source):
            low[...] = source[:2]
            high[...] = source[2:]

    @pl.when(g == 3)
    def _():
        low[...] = d_low[...]
        high[...] = d_high[...]


def product(rows, others, plane, w):
    low, high = rows
    other_low, other_high = others
    depth = low.shape[2]

    def pick(low, high):
        return jnp.where(plane < 2, low[plane % 2], high[plane % 2])

    x = jnp.dot(pick(low, high), w[:depth, :], preferred_element_type=jnp.float32)
    return x + jnp.dot(
        pick(other_low, other_high), w[depth:, :], preferred_element_type=jnp.float32
    )


def products(place, own, below, above, two, three, low, high, other_low, other_high, out):
    f, rows, other = place[1], (low, high), (other_low, other_high)
    total = (
        product(rows, other, f, own)
        + product(rows, other, jnp.maximum(f - 1, 0), below)
        + product(rows, other, jnp.minimum(f + 1, 3), above)
        + product(rows, other, f ^ 2, two)
        + product(rows, other, 3 - f, three)
    )
    out[1:] = total.reshape(3, -1, total.shape[1]).astype(jnp.bfloat16)


def attention(place, tiles, parts, q_ref, out_ref):
    g = place[0]
    groups_q = QH // KVH

    @pl.when(g == 0)
    def _():
        out_ref[...] = jnp.zeros_like(out_ref)

    @pl.when(g > 0)
    def _():
        kv = parts[0].astype(jnp.float32)
        for h in range(1, 4):
            kv = kv + parts[h].astype(jnp.float32)
        kv = kv.astype(jnp.bfloat16)
        slot = lax.broadcasted_iota(jnp.int32, (1, CAP), 1)
        for s in range(SAMP):
            live = slot < tiles[(g - 1) * SAMP + s] * TILE_TOK
            rows = slice(s * TXT_S, s * TXT_S + TXT_S)
            for k in range(kv.shape[1] // (2 * HD)):
                block = kv[s * CAP : s * CAP + CAP, k * 2 * HD : (k + 1) * 2 * HD]
                heads = [
                    slice((k * groups_q + j) * HD, (k * groups_q + j + 1) * HD)
                    for j in range(groups_q)
                ]
                query = jnp.concatenate([q_ref[rows, h] for h in heads], axis=0)
                scores = lax.dot_general(
                    query,
                    block[:, :HD],
                    (((1,), (1,)), ((), ())),
                    preferred_element_type=jnp.float32,
                ) * (1.0 / HD**0.5)
                scores = jnp.where(live, scores, -1e30)
                expo = jnp.exp(scores - jnp.max(scores, axis=-1, keepdims=True))
                weights = (expo / jnp.sum(expo, axis=-1, keepdims=True)).astype(jnp.bfloat16)
                out = jnp.dot(weights, block[:, HD:], preferred_element_type=jnp.float32)
                for j, h in enumerate(heads):
                    out_ref[rows, h] = out[j * TXT_S : (j + 1) * TXT_S].astype(jnp.bfloat16)


def shards_line(image_rows, enc_gain, key_value_w, tiles, queries):
    g, f, t = (lax.axis_index(a) for a in AXES)
    place = jnp.stack([g, f, t]).astype(jnp.int32)
    n_rows = image_rows.shape[0]
    per_group = n_rows // 3
    half = key_value_w.shape[1] // 2
    quarter = key_value_w.shape[0] // 4
    bf16, f32 = jnp.bfloat16, jnp.float32
    planes = range(4)

    def send(x, pairs):
        index = lambda p, c: (p[0] * 4 + p[1]) * 2 + c
        return lax.ppermute(x, AXES, [(index(a, c), index(b, c)) for a, b in pairs for c in (0, 1)])

    def swap(x):
        return lax.ppermute(x, "tp", [(0, 1), (1, 0)])

    w = lax.dynamic_slice_in_dim(key_value_w, g * quarter, quarter, axis=0)
    kept = lax.dynamic_slice_in_dim(w, t * half, half, axis=1)
    given = lax.dynamic_slice_in_dim(w, (1 - t) * half, half, axis=1)
    shape = (2 * quarter, half)
    own = call(join, [(shape, bf16)], kept, swap(given), specs=[VMEM, VMEM])[0]
    below = send(own, [((c, z), (c, z + 1)) for c in range(4) for z in range(3)])
    above = send(own, [((c, z + 1), (c, z)) for c in range(4) for z in range(3)])
    ready = call(onward, [(shape, bf16)], place, own, below, above, cost=COST)[0]
    pairs = ((0, 2), (3, 1), (2, 3), (1, 0))
    two = send(ready, [((c, a), (c, b)) for c in range(4) for a, b in pairs])
    three = send(two, [((c, a), (c, b)) for c in range(4) for a, b in pairs[2:]])

    x = image_rows.astype(f32)
    squares = jnp.sum(x * x, axis=1, keepdims=True)
    whole, part = ((4, n_rows, quarter), bf16), ((2, n_rows, quarter), bf16)
    a, b, c, d_low, d_high = call(
        normalise,
        [whole] * 3 + [part] * 2,
        place,
        image_rows,
        squares,
        swap(squares),
        enc_gain.reshape(1, -1),
    )
    to_b, to_c, to_d = ([((0, z), (h, z)) for z in planes] for h in (1, 2, 3))
    d_low, d_high = send(d_low, to_d), send(d_high, to_c)
    b, c = send(b, to_b), send(c, to_c)
    d_high = call(later, [part], d_high, ready, specs=[VMEM, ANY])[0]
    d_high = send(d_high, [((2, z), (3, z)) for z in planes])
    rows = call(landed, [part] * 2, place, a, b, c, d_low, d_high)
    rows = (*rows, *[swap(x) for x in rows])

    parts = ((4, per_group, half), bf16)
    parts = call(products, [parts], place, own, below, above, two, three, *rows)[0]
    parts = lax.all_to_all(parts, "grp", 0, 0, tiled=True)
    specs = [SMEM, SMEM, VMEM, VMEM]
    return call(attention, [(queries.shape, bf16)], place, tiles, parts, queries, specs=specs)[0]


def solution(mesh):
    sizes = tuple(mesh.shape[a] for a in AXES)
    return jax.shard_map(
        shards_line if sizes == (4, 4, 2) else shards_any,
        mesh=mesh,
        in_specs=(
            P(("grp", "fsdp"), "tp"),
            P("tp"),
            P(("tp", "fsdp"), None),
            P("fsdp"),
            P(("grp", "fsdp"), "tp"),
        ),
        out_specs=P(("grp", "fsdp"), "tp"),
        check_vma=False,
    )
```

```python
import jax
import jax.numpy as jnp
from jax import lax
from jax.experimental import pallas as pl
from jax.experimental.pallas import tpu as pltpu
from jax.sharding import PartitionSpec as P

D = 8192
HD = 128
KVH = 4
QH = 32
TILE_TOK = 16
SAMP = 2
TXT_S = 128
CAP = 64
AXES = ("grp", "fsdp", "tp")
VMEM = pl.BlockSpec(memory_space=pltpu.VMEM)
SMEM = pl.BlockSpec(memory_space=pltpu.SMEM)
ANY = pl.BlockSpec(memory_space=pl.ANY)
HBM = pl.BlockSpec(memory_space=pltpu.HBM)
LIMIT = 16 * 1024 * 1024
COST = 10


def attend_any(kv, tiles, queries, group):
    local_kv = kv.shape[1]
    groups_q = QH // KVH
    kv = kv.reshape(SAMP, CAP, local_kv, 2 * HD)
    keys = kv[..., :HD]
    values = kv[..., HD:]
    query = queries.reshape(SAMP, TXT_S, local_kv, groups_q, HD)
    counts = lax.dynamic_slice_in_dim(tiles, jnp.maximum(group - 1, 0) * SAMP, SAMP) * TILE_TOK
    live = jnp.arange(CAP)[None, :] < counts[:, None]
    scores = jnp.einsum("sikgd,sjkd->skgij", query, keys, preferred_element_type=jnp.float32) * (
        1.0 / HD**0.5
    )
    scores = jnp.where(live[:, None, None, None, :], scores, -1e30)
    top = jnp.max(scores, axis=-1, keepdims=True)
    expo = jnp.exp(scores - top)
    weights = (expo / jnp.sum(expo, axis=-1, keepdims=True)).astype(jnp.bfloat16)
    out = jnp.einsum(
        "skgij,sjkd->sikgd", weights, values, preferred_element_type=jnp.float32
    ).astype(jnp.bfloat16)
    out = jnp.where(group > 0, out, jnp.zeros_like(out))
    return out.reshape(queries.shape[0], queries.shape[1])


def shards_any(image_rows, enc_gain, key_value_w, tiles, queries):
    group = lax.axis_index("grp")
    per_group = image_rows.shape[0] // 3
    heads_kv = key_value_w.shape[1] // (2 * HD)
    rows = image_rows.astype(jnp.float32)
    squares = lax.psum(jnp.sum(rows * rows, axis=1, keepdims=True), "tp")
    normed = (rows * lax.rsqrt(squares / D + 1e-05) * enc_gain.astype(jnp.float32)).astype(
        jnp.bfloat16
    )
    parts = normed.reshape((3, per_group, normed.shape[1]))
    slots = jnp.concatenate([jnp.zeros_like(parts[:1]), parts], axis=0)
    mine = lax.all_to_all(slots, "grp", split_axis=0, concat_axis=0, tiled=True)[0]
    total = jnp.dot(
        mine,
        lax.all_gather(key_value_w, "fsdp", axis=0, tiled=True),
        preferred_element_type=jnp.float32,
    )
    heads = lax.psum_scatter(
        total.reshape(per_group, heads_kv, 2 * HD), "tp", scatter_dimension=1, tiled=True
    )
    return attend_any(heads.astype(jnp.bfloat16), tiles, queries, group)


def call(body, outs, *args, specs=None, out_spec=VMEM, cost=None, scratch=()):
    outs = [jax.ShapeDtypeStruct(s, d) for s, d in outs]
    if cost is not None:
        cost = pl.CostEstimate(flops=cost * 10**9, bytes_accessed=0, transcendentals=0)
    return pl.pallas_call(
        body,
        out_shape=outs,
        in_specs=specs or [SMEM] + [VMEM] * (len(args) - 1),
        out_specs=[out_spec] * len(outs),
        cost_estimate=cost,
        scratch_shapes=list(scratch),
        compiler_params=pltpu.CompilerParams(vmem_limit_bytes=LIMIT),
    )(*args)


def join(kept, other, out):
    rows = kept.shape[0]
    out[:rows, :] = kept[...]
    out[rows:, :] = other[...]


def row_squares(place, x, squares):
    @pl.when(place[0] == 0)
    def _():
        total = None
        for col in range(0, x.shape[1], 128):
            part = x[:, col : col + 128].astype(jnp.float32)
            total = part * part if total is None else total + part * part
        squares[...] = total


def normalise(place, x, squares, other, gain, a, b, c, d_low, d_high):
    width = x.shape[1] // 16

    @pl.when(place[0] == 0)
    def _():
        total = jnp.sum(squares[...] + other[...], axis=1, keepdims=True)
        scale = lax.rsqrt(total / D + 1e-05)
        for z in range(4):
            for h in range(4):
                cols = slice((z * 4 + h) * width, (z * 4 + h + 1) * width)
                y = x[:, cols].astype(jnp.float32) * scale * gain[:, cols].astype(jnp.float32)
                out, at = ((a, b, c)[h], z) if h < 3 else ((d_low, d_high)[z // 2], z % 2)
                out[at] = y.astype(jnp.bfloat16)


def onward(place, own, middle, near, out, sem):
    del near
    end = (place[1] == 0) | (place[1] == 3)
    for use, source in ((end, own), (jnp.logical_not(end), middle)):

        @pl.when(use)
        def _(source=source):
            copy = pltpu.make_async_copy(source, out, sem)
            copy.start()
            copy.wait()


def later(x, after, out):
    del after
    out[...] = x[...]


def landed(place, a, b, c, d_low, d_high, low, high):
    g = place[0]
    for who, source in ((0, a), (1, b), (2, c)):

        @pl.when(g == who)
        def _(source=source):
            low[...] = source[:2]
            high[...] = source[2:]

    @pl.when(g == 3)
    def _():
        low[...] = d_low[...]
        high[...] = d_high[...]


def products(place, own, near, middle, two, *refs):
    rows, total = refs[:4], refs[4]
    depth = rows[0].shape[2]
    for f in range(4):
        planes = {f: own, f ^ 1: near, f ^ 2: two}
        if f in (1, 2):
            planes[3 - f] = middle

        @pl.when(place[1] == f)
        def _(planes=planes):
            out = None
            for z, w in planes.items():
                for core in range(2):
                    y = jnp.dot(
                        rows[2 * core + z // 2][z % 2],
                        w[core * depth : (core + 1) * depth, :],
                        preferred_element_type=jnp.float32,
                    )
                    out = y if out is None else out + y
            total[...] = out


def last_product(place, three, *refs):
    rows, (total, mine, one, two, other, held) = refs[:4], refs[4:]
    depth = rows[0].shape[2]
    g, n = place[0], mine.shape[0]

    def put(x):
        held[...] = x
        for k, out in enumerate((mine, one, two, other)):
            at = pl.multiple_of(jnp.maximum((g ^ k) - 1, 0) * n, n)
            out[...] = held[pl.ds(at, n), :].astype(out.dtype)

    for f in (0, 3):

        @pl.when(place[1] == f)
        def _(z=3 - f):
            x = total[...]
            for core in range(2):
                x = x + jnp.dot(
                    rows[2 * core + z // 2][z % 2],
                    three[core * depth : (core + 1) * depth, :],
                    preferred_element_type=jnp.float32,
                )
            put(x)

    @pl.when((place[1] == 1) | (place[1] == 2))
    def _():
        put(total[...])


def attention(place, tiles, mine, one, two, three, q_ref, out_ref, held, sems):
    g = place[0]
    groups_q = QH // KVH
    copies = [
        pltpu.make_async_copy(held.at[at, :], out_ref.at[at, :], sems.at[s])
        for s, at in enumerate(pl.ds(s * TXT_S, TXT_S) for s in range(SAMP))
    ]

    @pl.when(g == 0)
    def _():
        held[...] = jnp.zeros_like(held)
        for copy in copies:
            copy.start()

    @pl.when(g > 0)
    def _():
        kv = mine[...]
        for part in (one, two, three):
            kv = kv + part[...].astype(jnp.float32)
        kv = kv.astype(jnp.bfloat16)
        slot = lax.broadcasted_iota(jnp.int32, (CAP, 1), 0)
        for s, copy in enumerate(copies):
            live = slot < tiles[(g - 1) * SAMP + s] * TILE_TOK
            rows = slice(s * TXT_S, s * TXT_S + TXT_S)
            for k in range(kv.shape[1] // (2 * HD)):
                block = kv[s * CAP : s * CAP + CAP, k * 2 * HD : (k + 1) * 2 * HD]
                heads = [
                    slice((k * groups_q + j) * HD, (k * groups_q + j + 1) * HD)
                    for j in range(groups_q)
                ]
                query = jnp.concatenate([q_ref[rows, h] for h in heads], axis=0)
                scores = lax.dot_general(
                    block[:, :HD],
                    query,
                    (((1,), (1,)), ((), ())),
                    preferred_element_type=jnp.float32,
                ) * (1.0 / HD**0.5)
                scores = jnp.where(live, scores, -1e30)
                expo = jnp.exp(scores - jnp.max(scores, axis=0, keepdims=True))
                weights = (expo / jnp.sum(expo, axis=0, keepdims=True)).astype(jnp.bfloat16)
                out = lax.dot_general(
                    weights,
                    block[:, HD:],
                    (((0,), (0,)), ((), ())),
                    preferred_element_type=jnp.float32,
                )
                for j, h in enumerate(heads):
                    held[rows, h] = out[j * TXT_S : (j + 1) * TXT_S].astype(jnp.bfloat16)
            copy.start()

    for copy in copies:
        copy.wait()


def shards_line(image_rows, enc_gain, key_value_w, tiles, queries):
    g, f, t = (lax.axis_index(a) for a in AXES)
    place = jnp.stack([g, f, t]).astype(jnp.int32)
    n_rows = image_rows.shape[0]
    per_group = n_rows // 3
    half = key_value_w.shape[1] // 2
    quarter = key_value_w.shape[0] // 4
    bf16, f32 = jnp.bfloat16, jnp.float32
    planes = range(4)

    def send(x, pairs):
        index = lambda p, c: (p[0] * 4 + p[1]) * 2 + c
        return lax.ppermute(x, AXES, [(index(a, c), index(b, c)) for a, b in pairs for c in (0, 1)])

    def swap(x):
        return lax.ppermute(x, "tp", [(0, 1), (1, 0)])

    w = lax.dynamic_slice_in_dim(key_value_w, g * quarter, quarter, axis=0)
    kept = lax.dynamic_slice_in_dim(w, t * half, half, axis=1)
    given = lax.dynamic_slice_in_dim(w, (1 - t) * half, half, axis=1)
    shape = (2 * quarter, half)
    own = call(join, [(shape, bf16)], kept, swap(given), specs=[VMEM, VMEM])[0]
    middle = send(own, [((c, z), (c, 3 - z)) for c in range(4) for z in (1, 2)])
    near = send(own, [((c, z), (c, z ^ 1)) for c in range(4) for z in planes])
    ready = call(
        onward,
        [(shape, bf16)],
        place,
        own,
        middle,
        near,
        specs=[SMEM] + [ANY] * 3,
        cost=COST,
        scratch=[pltpu.SemaphoreType.DMA],
    )[0]
    pairs = ((0, 2), (3, 1), (2, 3), (1, 0))
    two = send(ready, [((c, a), (c, b)) for c in range(4) for a, b in pairs])
    three = send(two, [((c, a), (c, b)) for c in range(4) for a, b in pairs[2:]])

    squares = call(row_squares, [((n_rows, 128), f32)], place, image_rows)[0]
    whole, part = ((4, n_rows, quarter), bf16), ((2, n_rows, quarter), bf16)
    a, b, c, d_low, d_high = call(
        normalise,
        [whole] * 3 + [part] * 2,
        place,
        image_rows,
        squares,
        swap(squares),
        enc_gain.reshape(1, -1),
    )
    to_b, to_c, to_d = ([((0, z), (h, z)) for z in planes] for h in (1, 2, 3))
    d_low, d_high = send(d_low, to_d), send(d_high, to_c)
    b, c = send(b, to_b), send(c, to_c)
    d_high = call(later, [part], d_high, ready, specs=[VMEM, ANY])[0]
    d_high = send(d_high, [((2, z), (3, z)) for z in planes])
    rows = call(landed, [part] * 2, place, a, b, c, d_low, d_high)
    rows = (*rows, *[swap(x) for x in rows])

    total = call(products, [((n_rows, half), f32)], place, own, near, middle, two, *rows)[0]
    message = (per_group, half)
    mine, *parts = call(
        last_product,
        [(message, f32)] + [(message, bf16)] * 3,
        place,
        three,
        *rows,
        total,
        scratch=[pltpu.VMEM((n_rows, half), f32)],
    )
    parts = [
        send(x, [((c, z), (c ^ k, z)) for c in range(4) for z in planes])
        for k, x in zip((1, 2, 3), parts)
    ]
    return call(
        attention,
        [(queries.shape, bf16)],
        place,
        tiles,
        mine,
        *parts,
        queries,
        specs=[SMEM] * 2 + [VMEM] * 5,
        out_spec=ANY,
        scratch=[pltpu.VMEM(queries.shape, bf16), pltpu.SemaphoreType.DMA((SAMP,))],
    )[0]


def solution(mesh):
    sizes = tuple(mesh.shape[a] for a in AXES)
    return jax.shard_map(
        shards_line if sizes == (4, 4, 2) else shards_any,
        mesh=mesh,
        in_specs=(
            P(("grp", "fsdp"), "tp"),
            P("tp"),
            P(("tp", "fsdp"), None),
            P("fsdp"),
            P(("grp", "fsdp"), "tp"),
        ),
        out_specs=P(("grp", "fsdp"), "tp"),
        check_vma=False,
    )
```

```python
import jax
import jax.numpy as jnp
from jax import lax
from jax.experimental import pallas as pl
from jax.experimental.pallas import tpu as pltpu
from jax.sharding import PartitionSpec as P

D = 8192
HD = 128
KVH = 4
QH = 32
TILE_TOK = 16
SAMP = 2
TXT_S = 128
CAP = 64
AXES = ("grp", "fsdp", "tp")
VMEM = pl.BlockSpec(memory_space=pltpu.VMEM)
ANY = pl.BlockSpec(memory_space=pl.ANY)
HBM = pl.BlockSpec(memory_space=pltpu.HBM)
LIMIT = 16 * 1024 * 1024
COST = 10


def attend_any(kv, tiles, queries, group):
    local_kv = kv.shape[1]
    groups_q = QH // KVH
    kv = kv.reshape(SAMP, CAP, local_kv, 2 * HD)
    keys = kv[..., :HD]
    values = kv[..., HD:]
    query = queries.reshape(SAMP, TXT_S, local_kv, groups_q, HD)
    counts = lax.dynamic_slice_in_dim(tiles, jnp.maximum(group - 1, 0) * SAMP, SAMP) * TILE_TOK
    live = jnp.arange(CAP)[None, :] < counts[:, None]
    scores = jnp.einsum("sikgd,sjkd->skgij", query, keys, preferred_element_type=jnp.float32) * (
        1.0 / HD**0.5
    )
    scores = jnp.where(live[:, None, None, None, :], scores, -1e30)
    top = jnp.max(scores, axis=-1, keepdims=True)
    expo = jnp.exp(scores - top)
    weights = (expo / jnp.sum(expo, axis=-1, keepdims=True)).astype(jnp.bfloat16)
    out = jnp.einsum(
        "skgij,sjkd->sikgd", weights, values, preferred_element_type=jnp.float32
    ).astype(jnp.bfloat16)
    out = jnp.where(group > 0, out, jnp.zeros_like(out))
    return out.reshape(queries.shape[0], queries.shape[1])


def shards_any(image_rows, enc_gain, key_value_w, tiles, queries):
    group = lax.axis_index("grp")
    per_group = image_rows.shape[0] // 3
    heads_kv = key_value_w.shape[1] // (2 * HD)
    rows = image_rows.astype(jnp.float32)
    squares = lax.psum(jnp.sum(rows * rows, axis=1, keepdims=True), "tp")
    normed = (rows * lax.rsqrt(squares / D + 1e-05) * enc_gain.astype(jnp.float32)).astype(
        jnp.bfloat16
    )
    parts = normed.reshape((3, per_group, normed.shape[1]))
    slots = jnp.concatenate([jnp.zeros_like(parts[:1]), parts], axis=0)
    mine = lax.all_to_all(slots, "grp", split_axis=0, concat_axis=0, tiled=True)[0]
    total = jnp.dot(
        mine,
        lax.all_gather(key_value_w, "fsdp", axis=0, tiled=True),
        preferred_element_type=jnp.float32,
    )
    heads = lax.psum_scatter(
        total.reshape(per_group, heads_kv, 2 * HD), "tp", scatter_dimension=1, tiled=True
    )
    return attend_any(heads.astype(jnp.bfloat16), tiles, queries, group)


def call(body, outs, *args, specs=None, out_spec=VMEM, cost=None, scratch=()):
    outs = [jax.ShapeDtypeStruct(s, d) for s, d in outs]
    if cost is not None:
        cost = pl.CostEstimate(flops=cost * 10**9, bytes_accessed=0, transcendentals=0)
    return pl.pallas_call(
        body,
        out_shape=outs,
        in_specs=specs or [VMEM] * len(args),
        out_specs=[out_spec] * len(outs),
        cost_estimate=cost,
        scratch_shapes=list(scratch),
        compiler_params=pltpu.CompilerParams(vmem_limit_bytes=LIMIT),
    )(*args)


def join(kept, other, out):
    rows = kept.shape[0]
    out[:rows, :] = kept[...]
    out[rows:, :] = other[...]


def row_squares(x, squares):
    @pl.when(lax.axis_index("grp") == 0)
    def _():
        total = None
        for col in range(0, x.shape[1], 128):
            part = x[:, col : col + 128].astype(jnp.float32)
            total = part * part if total is None else total + part * part
        squares[...] = total


def normalise(x, squares, other, gain, a, b, c, d_low, d_high):
    width = x.shape[1] // 16

    @pl.when(lax.axis_index("grp") == 0)
    def _():
        total = jnp.sum(squares[...] + other[...], axis=1, keepdims=True)
        scale = lax.rsqrt(total / D + 1e-05)
        for z in range(4):
            for h in range(4):
                cols = slice((z * 4 + h) * width, (z * 4 + h + 1) * width)
                y = x[:, cols].astype(jnp.float32) * scale * gain[:, cols].astype(jnp.float32)
                out, at = ((a, b, c)[h], z) if h < 3 else ((d_low, d_high)[z // 2], z % 2)
                out[at] = y.astype(jnp.bfloat16)


def later(x, *rest):
    rest[-1][...] = x[...]


def landed(a, b, c, d_low, d_high, low, high):
    g = lax.axis_index("grp")
    for who, source in ((0, a), (1, b), (2, c)):

        @pl.when(g == who)
        def _(source=source):
            low[...] = source[:2]
            high[...] = source[2:]

    @pl.when(g == 3)
    def _():
        low[...] = d_low[...]
        high[...] = d_high[...]


def add_products(rows, blocks, total):
    depth = rows[0].shape[2]
    for f in range(4):

        @pl.when(lax.axis_index("fsdp") == f)
        def _(f=f):
            out = None
            for k, w in blocks.items():
                z = f ^ k
                for core in range(2):
                    y = jnp.dot(
                        rows[2 * core + z // 2][z % 2],
                        w[core * depth : (core + 1) * depth, :],
                        preferred_element_type=jnp.float32,
                    )
                    out = y if out is None else out + y
            total(out)


def products(own, near, far, *refs):
    def put(x):
        refs[4][...] = x

    add_products(refs[:4], {0: own, 1: near, 2: far}, put)


def last_product(last, *refs):
    rows, (total, mine, one, two, other, held) = refs[:4], refs[4:]
    g, n = lax.axis_index("grp"), mine.shape[0]

    def put(x):
        held[...] = total[...] + x

    add_products(rows, {3: last}, put)
    for k, out in enumerate((mine, one, two, other)):
        at = pl.multiple_of(jnp.maximum((g ^ k) - 1, 0) * n, n)
        out[...] = held[pl.ds(at, n), :].astype(out.dtype)


def attention(counts, mine, one, two, three, q_ref, out_ref, held, sems):
    g = lax.axis_index("grp")
    groups_q = QH // KVH
    copies = [
        pltpu.make_async_copy(held.at[at, :], out_ref.at[at, :], sems.at[s])
        for s, at in enumerate(pl.ds(s * TXT_S, TXT_S) for s in range(SAMP))
    ]

    @pl.when(g == 0)
    def _():
        held[...] = jnp.zeros_like(held)
        for copy in copies:
            copy.start()

    @pl.when(g > 0)
    def _():
        kv = mine[...]
        for part in (one, two, three):
            kv = kv + part[...].astype(jnp.float32)
        kv = kv.astype(jnp.bfloat16)
        slot = lax.broadcasted_iota(jnp.int32, (CAP, 1), 0)
        for s, copy in enumerate(copies):
            live = slot < counts[s : s + 1, :1]
            rows = slice(s * TXT_S, s * TXT_S + TXT_S)
            for k in range(kv.shape[1] // (2 * HD)):
                block = kv[s * CAP : s * CAP + CAP, k * 2 * HD : (k + 1) * 2 * HD]
                heads = [
                    slice((k * groups_q + j) * HD, (k * groups_q + j + 1) * HD)
                    for j in range(groups_q)
                ]
                query = jnp.concatenate([q_ref[rows, h] for h in heads], axis=0)
                scores = lax.dot_general(
                    block[:, :HD],
                    query,
                    (((1,), (1,)), ((), ())),
                    preferred_element_type=jnp.float32,
                ) * (1.0 / HD**0.5)
                scores = jnp.where(live, scores, -1e30)
                expo = jnp.exp(scores - jnp.max(scores, axis=0, keepdims=True))
                weights = (expo / jnp.sum(expo, axis=0, keepdims=True)).astype(jnp.bfloat16)
                out = lax.dot_general(
                    weights,
                    block[:, HD:],
                    (((0,), (0,)), ((), ())),
                    preferred_element_type=jnp.float32,
                )
                for j, h in enumerate(heads):
                    held[rows, h] = out[j * TXT_S : (j + 1) * TXT_S].astype(jnp.bfloat16)
            copy.start()

    for copy in copies:
        copy.wait()


def shards_line(image_rows, enc_gain, key_value_w, tiles, queries):
    g, t = lax.axis_index("grp"), lax.axis_index("tp")
    n_rows = image_rows.shape[0]
    per_group = n_rows // 3
    half = key_value_w.shape[1] // 2
    quarter = key_value_w.shape[0] // 4
    bf16, f32 = jnp.bfloat16, jnp.float32
    planes = range(4)

    def send(x, pairs):
        index = lambda p, c: (p[0] * 4 + p[1]) * 2 + c
        return lax.ppermute(x, AXES, [(index(a, c), index(b, c)) for a, b in pairs for c in (0, 1)])

    def swap(x):
        return lax.ppermute(x, "tp", [(0, 1), (1, 0)])

    w = lax.dynamic_slice_in_dim(key_value_w, g * quarter, quarter, axis=0)
    kept = lax.dynamic_slice_in_dim(w, t * half, half, axis=1)
    given = lax.dynamic_slice_in_dim(w, (1 - t) * half, half, axis=1)
    shape = (2 * quarter, half)
    own = call(join, [(shape, bf16)], kept, swap(given), cost=1)[0]

    def swap_planes(x, k):
        return send(x, [((c, z), (c, z ^ k)) for c in range(4) for z in planes])

    near, far = swap_planes(own, 1), swap_planes(own, 2)

    squares = call(row_squares, [((n_rows, 128), f32)], image_rows)[0]
    whole, part = ((4, n_rows, quarter), bf16), ((2, n_rows, quarter), bf16)
    a, b, c, d_low, d_high = call(
        normalise,
        [whole] * 3 + [part] * 2,
        image_rows,
        squares,
        swap(squares),
        enc_gain.reshape(1, -1),
    )
    to_b, to_c, to_d = ([((0, z), (h, z)) for z in planes] for h in (1, 2, 3))
    d_low, d_high = send(d_low, to_d), send(d_high, to_c)
    b, c = send(b, to_b), send(c, to_c)
    last = call(later, [(shape, bf16)], far, near, d_low, specs=[VMEM, ANY, ANY], cost=COST)[0]
    last = swap_planes(last, 1)
    d_high = send(d_high, [((2, z), (3, z)) for z in planes])
    rows = call(landed, [part] * 2, a, b, c, d_low, d_high)
    rows = (*rows, *[swap(x) for x in rows])

    total = call(products, [((n_rows, half), f32)], own, near, far, *rows)[0]
    counts = lax.dynamic_slice_in_dim(tiles, jnp.maximum(g - 1, 0) * SAMP, SAMP) * TILE_TOK
    message = (per_group, half)
    mine, *parts = call(
        last_product,
        [(message, f32)] + [(message, bf16)] * 3,
        last,
        *rows,
        total,
        scratch=[pltpu.VMEM((n_rows, half), f32)],
    )
    parts = [
        send(x, [((c, z), (c ^ k, z)) for c in range(4) for z in planes])
        for k, x in zip((1, 2, 3), parts)
    ]
    return call(
        attention,
        [(queries.shape, bf16)],
        jnp.broadcast_to(counts[:, None], (SAMP, 128)),
        mine,
        *parts,
        queries,
        out_spec=ANY,
        scratch=[pltpu.VMEM(queries.shape, bf16), pltpu.SemaphoreType.DMA((SAMP,))],
    )[0]


def solution(mesh):
    sizes = tuple(mesh.shape[a] for a in AXES)
    return jax.shard_map(
        shards_line if sizes == (4, 4, 2) else shards_any,
        mesh=mesh,
        in_specs=(
            P(("grp", "fsdp"), "tp"),
            P("tp"),
            P(("tp", "fsdp"), None),
            P("fsdp"),
            P(("grp", "fsdp"), "tp"),
        ),
        out_specs=P(("grp", "fsdp"), "tp"),
        check_vma=False,
    )
```

```python
import jax
import jax.numpy as jnp
from jax import lax
from jax.experimental import pallas as pl
from jax.experimental.pallas import tpu as pltpu
from jax.sharding import PartitionSpec as P

D = 8192
HD = 128
KVH = 4
QH = 32
TILE_TOK = 16
SAMP = 2
TXT_S = 128
CAP = 64
AXES = ("grp", "fsdp", "tp")
VMEM = pl.BlockSpec(memory_space=pltpu.VMEM)
ANY = pl.BlockSpec(memory_space=pl.ANY)
HBM = pl.BlockSpec(memory_space=pltpu.HBM)
LIMIT = 16 * 1024 * 1024
COST = 10


def attend_any(kv, tiles, queries, group):
    local_kv = kv.shape[1]
    groups_q = QH // KVH
    kv = kv.reshape(SAMP, CAP, local_kv, 2 * HD)
    keys = kv[..., :HD]
    values = kv[..., HD:]
    query = queries.reshape(SAMP, TXT_S, local_kv, groups_q, HD)
    counts = lax.dynamic_slice_in_dim(tiles, jnp.maximum(group - 1, 0) * SAMP, SAMP) * TILE_TOK
    live = jnp.arange(CAP)[None, :] < counts[:, None]
    scores = jnp.einsum("sikgd,sjkd->skgij", query, keys, preferred_element_type=jnp.float32) * (
        1.0 / HD**0.5
    )
    scores = jnp.where(live[:, None, None, None, :], scores, -1e30)
    top = jnp.max(scores, axis=-1, keepdims=True)
    expo = jnp.exp(scores - top)
    weights = (expo / jnp.sum(expo, axis=-1, keepdims=True)).astype(jnp.bfloat16)
    out = jnp.einsum(
        "skgij,sjkd->sikgd", weights, values, preferred_element_type=jnp.float32
    ).astype(jnp.bfloat16)
    out = jnp.where(group > 0, out, jnp.zeros_like(out))
    return out.reshape(queries.shape[0], queries.shape[1])


def shards_any(image_rows, enc_gain, key_value_w, tiles, queries):
    group = lax.axis_index("grp")
    per_group = image_rows.shape[0] // 3
    heads_kv = key_value_w.shape[1] // (2 * HD)
    rows = image_rows.astype(jnp.float32)
    squares = lax.psum(jnp.sum(rows * rows, axis=1, keepdims=True), "tp")
    normed = (rows * lax.rsqrt(squares / D + 1e-05) * enc_gain.astype(jnp.float32)).astype(
        jnp.bfloat16
    )
    parts = normed.reshape((3, per_group, normed.shape[1]))
    slots = jnp.concatenate([jnp.zeros_like(parts[:1]), parts], axis=0)
    mine = lax.all_to_all(slots, "grp", split_axis=0, concat_axis=0, tiled=True)[0]
    total = jnp.dot(
        mine,
        lax.all_gather(key_value_w, "fsdp", axis=0, tiled=True),
        preferred_element_type=jnp.float32,
    )
    heads = lax.psum_scatter(
        total.reshape(per_group, heads_kv, 2 * HD), "tp", scatter_dimension=1, tiled=True
    )
    return attend_any(heads.astype(jnp.bfloat16), tiles, queries, group)


def call(body, outs, *args, specs=None, out_spec=VMEM, cost=None, scratch=()):
    outs = [jax.ShapeDtypeStruct(s, d) for s, d in outs]
    if cost is not None:
        cost = pl.CostEstimate(flops=cost * 10**9, bytes_accessed=0, transcendentals=0)
    return pl.pallas_call(
        body,
        out_shape=outs,
        in_specs=specs or [VMEM] * len(args),
        out_specs=[out_spec] * len(outs),
        cost_estimate=cost,
        scratch_shapes=list(scratch),
        compiler_params=pltpu.CompilerParams(vmem_limit_bytes=LIMIT),
    )(*args)


def join(kept, other, out):
    rows = kept.shape[0]
    out[:rows, :] = kept[...]
    out[rows:, :] = other[...]


def row_squares(x, after, squares):
    del after

    @pl.when(lax.axis_index("grp") == 0)
    def _():
        total = None
        for col in range(0, x.shape[1], 128):
            part = x[:, col : col + 128].astype(jnp.float32)
            total = part * part if total is None else total + part * part
        squares[...] = total


def normalise(x, squares, other, gain, a, b, c, d_low, d_high):
    width = x.shape[1] // 16

    @pl.when(lax.axis_index("grp") == 0)
    def _():
        total = jnp.sum(squares[...] + other[...], axis=1, keepdims=True)
        scale = lax.rsqrt(total / D + 1e-05)
        for z in range(4):
            for h in range(4):
                cols = slice((z * 4 + h) * width, (z * 4 + h + 1) * width)
                y = x[:, cols].astype(jnp.float32) * scale * gain[:, cols].astype(jnp.float32)
                out, at = ((a, b, c)[h], z) if h < 3 else ((d_low, d_high)[z // 2], z % 2)
                out[at] = y.astype(jnp.bfloat16)


def later(x, *rest):
    rest[-1][...] = x[...]


def landed(a, b, c, d_low, d_high, low, high):
    g = lax.axis_index("grp")
    for who, source in ((0, a), (1, b), (2, c)):

        @pl.when(g == who)
        def _(source=source):
            low[...] = source[:2]
            high[...] = source[2:]

    @pl.when(g == 3)
    def _():
        low[...] = d_low[...]
        high[...] = d_high[...]


def add_products(rows, blocks, total):
    depth = rows[0].shape[2]
    for f in range(4):

        @pl.when(lax.axis_index("fsdp") == f)
        def _(f=f):
            out = None
            for k, w in blocks.items():
                z = f ^ k
                for core in range(2):
                    y = jnp.dot(
                        rows[2 * core + z // 2][z % 2],
                        w[core * depth : (core + 1) * depth, :],
                        preferred_element_type=jnp.float32,
                    )
                    out = y if out is None else out + y
            total(out)


def products(own, near, far, *refs):
    def put(x):
        refs[4][...] = x

    add_products(refs[:4], {0: own, 1: near, 2: far}, put)


def last_product(last, *refs):
    rows, (total, mine, one, two, other, held) = refs[:4], refs[4:]
    g, n = lax.axis_index("grp"), mine.shape[0]

    def put(x):
        held[...] = total[...] + x

    add_products(rows, {3: last}, put)
    for k, out in enumerate((mine, one, two, other)):
        at = pl.multiple_of(jnp.maximum((g ^ k) - 1, 0) * n, n)
        out[...] = held[pl.ds(at, n), :].astype(out.dtype)


def attention(counts, mine, one, two, three, q_ref, out_ref, held, sems):
    g = lax.axis_index("grp")
    groups_q = QH // KVH
    copies = [
        pltpu.make_async_copy(held.at[at, :], out_ref.at[at, :], sems.at[s])
        for s, at in enumerate(pl.ds(s * TXT_S, TXT_S) for s in range(SAMP))
    ]

    @pl.when(g == 0)
    def _():
        held[...] = jnp.zeros_like(held)
        for copy in copies:
            copy.start()

    @pl.when(g > 0)
    def _():
        kv = mine[...]
        for part in (one, two, three):
            kv = kv + part[...].astype(jnp.float32)
        kv = kv.astype(jnp.bfloat16)
        slot = lax.broadcasted_iota(jnp.int32, (CAP, 1), 0)
        for s, copy in enumerate(copies):
            live = slot < counts[s : s + 1, :1]
            rows = slice(s * TXT_S, s * TXT_S + TXT_S)
            for k in range(kv.shape[1] // (2 * HD)):
                block = kv[s * CAP : s * CAP + CAP, k * 2 * HD : (k + 1) * 2 * HD]
                heads = [
                    slice((k * groups_q + j) * HD, (k * groups_q + j + 1) * HD)
                    for j in range(groups_q)
                ]
                query = jnp.concatenate([q_ref[rows, h] for h in heads], axis=0)
                scores = lax.dot_general(
                    block[:, :HD],
                    query,
                    (((1,), (1,)), ((), ())),
                    preferred_element_type=jnp.float32,
                ) * (1.0 / HD**0.5)
                scores = jnp.where(live, scores, -1e30)
                expo = jnp.exp(scores - jnp.max(scores, axis=0, keepdims=True))
                weights = (expo / jnp.sum(expo, axis=0, keepdims=True)).astype(jnp.bfloat16)
                out = lax.dot_general(
                    weights,
                    block[:, HD:],
                    (((0,), (0,)), ((), ())),
                    preferred_element_type=jnp.float32,
                )
                for j, h in enumerate(heads):
                    held[rows, h] = out[j * TXT_S : (j + 1) * TXT_S].astype(jnp.bfloat16)
            copy.start()

    for copy in copies:
        copy.wait()


def shards_line(image_rows, enc_gain, key_value_w, tiles, queries):
    g, t = lax.axis_index("grp"), lax.axis_index("tp")
    n_rows = image_rows.shape[0]
    per_group = n_rows // 3
    half = key_value_w.shape[1] // 2
    quarter = key_value_w.shape[0] // 4
    bf16, f32 = jnp.bfloat16, jnp.float32
    planes = range(4)

    def send(x, pairs):
        index = lambda p, c: (p[0] * 4 + p[1]) * 2 + c
        return lax.ppermute(x, AXES, [(index(a, c), index(b, c)) for a, b in pairs for c in (0, 1)])

    def swap(x):
        return lax.ppermute(x, "tp", [(0, 1), (1, 0)])

    w = lax.dynamic_slice_in_dim(key_value_w, g * quarter, quarter, axis=0)
    kept = lax.dynamic_slice_in_dim(w, t * half, half, axis=1)
    given = lax.dynamic_slice_in_dim(w, (1 - t) * half, half, axis=1)
    shape = (2 * quarter, half)
    own = call(join, [(shape, bf16)], kept, swap(given), cost=1)[0]

    def swap_planes(x, k):
        return send(x, [((c, z), (c, z ^ k)) for c in range(4) for z in planes])

    near, far = swap_planes(own, 1), swap_planes(own, 2)

    squares = call(row_squares, [((n_rows, 128), f32)], image_rows, own, specs=[VMEM, ANY])[0]
    whole, part = ((4, n_rows, quarter), bf16), ((2, n_rows, quarter), bf16)
    a, b, c, d_low, d_high = call(
        normalise,
        [whole] * 3 + [part] * 2,
        image_rows,
        squares,
        swap(squares),
        enc_gain.reshape(1, -1),
    )
    to_b, to_c, to_d = ([((0, z), (h, z)) for z in planes] for h in (1, 2, 3))
    d_low, d_high = send(d_low, to_d), send(d_high, to_c)
    c = call(later, [whole], c, d_low, specs=[VMEM, ANY], cost=0)[0]
    b, c = send(b, to_b), send(c, to_c)
    last = call(later, [(shape, bf16)], far, near, specs=[VMEM, ANY], cost=COST)[0]
    last = swap_planes(last, 1)
    d_high = send(d_high, [((2, z), (3, z)) for z in planes])
    rows = call(landed, [part] * 2, a, b, c, d_low, d_high)
    rows = (*rows, *[swap(x) for x in rows])

    total = call(products, [((n_rows, half), f32)], own, near, far, *rows)[0]
    counts = lax.dynamic_slice_in_dim(tiles, jnp.maximum(g - 1, 0) * SAMP, SAMP) * TILE_TOK
    message = (per_group, half)
    mine, *parts = call(
        last_product,
        [(message, f32)] + [(message, bf16)] * 3,
        last,
        *rows,
        total,
        scratch=[pltpu.VMEM((n_rows, half), f32)],
    )
    parts = [
        send(x, [((c, z), (c ^ k, z)) for c in range(4) for z in planes])
        for k, x in zip((3, 1, 2), (parts[2], parts[0], parts[1]))
    ]
    return call(
        attention,
        [(queries.shape, bf16)],
        jnp.broadcast_to(counts[:, None], (SAMP, 128)),
        mine,
        *parts,
        queries,
        out_spec=ANY,
        scratch=[pltpu.VMEM(queries.shape, bf16), pltpu.SemaphoreType.DMA((SAMP,))],
    )[0]


def solution(mesh):
    sizes = tuple(mesh.shape[a] for a in AXES)
    return jax.shard_map(
        shards_line if sizes == (4, 4, 2) else shards_any,
        mesh=mesh,
        in_specs=(
            P(("grp", "fsdp"), "tp"),
            P("tp"),
            P(("tp", "fsdp"), None),
            P("fsdp"),
            P(("grp", "fsdp"), "tp"),
        ),
        out_specs=P(("grp", "fsdp"), "tp"),
        check_vma=False,
    )
```

```python
import jax
import jax.numpy as jnp
from jax import lax
from jax.experimental import pallas as pl
from jax.experimental.pallas import tpu as pltpu
from jax.sharding import PartitionSpec as P

D = 8192
HD = 128
KVH = 4
QH = 32
TILE_TOK = 16
SAMP = 2
TXT_S = 128
CAP = 64
AXES = ("grp", "fsdp", "tp")
VMEM = pl.BlockSpec(memory_space=pltpu.VMEM)
ANY = pl.BlockSpec(memory_space=pl.ANY)
HBM = pl.BlockSpec(memory_space=pltpu.HBM)
LIMIT = 16 * 1024 * 1024
COST = 10
EARLY = 10


def attend_any(kv, tiles, queries, group):
    local_kv = kv.shape[1]
    groups_q = QH // KVH
    kv = kv.reshape(SAMP, CAP, local_kv, 2 * HD)
    keys = kv[..., :HD]
    values = kv[..., HD:]
    query = queries.reshape(SAMP, TXT_S, local_kv, groups_q, HD)
    counts = lax.dynamic_slice_in_dim(tiles, jnp.maximum(group - 1, 0) * SAMP, SAMP) * TILE_TOK
    live = jnp.arange(CAP)[None, :] < counts[:, None]
    scores = jnp.einsum("sikgd,sjkd->skgij", query, keys, preferred_element_type=jnp.float32) * (
        1.0 / HD**0.5
    )
    scores = jnp.where(live[:, None, None, None, :], scores, -1e30)
    top = jnp.max(scores, axis=-1, keepdims=True)
    expo = jnp.exp(scores - top)
    weights = (expo / jnp.sum(expo, axis=-1, keepdims=True)).astype(jnp.bfloat16)
    out = jnp.einsum(
        "skgij,sjkd->sikgd", weights, values, preferred_element_type=jnp.float32
    ).astype(jnp.bfloat16)
    out = jnp.where(group > 0, out, jnp.zeros_like(out))
    return out.reshape(queries.shape[0], queries.shape[1])


def shards_any(image_rows, enc_gain, key_value_w, tiles, queries):
    group = lax.axis_index("grp")
    per_group = image_rows.shape[0] // 3
    heads_kv = key_value_w.shape[1] // (2 * HD)
    rows = image_rows.astype(jnp.float32)
    squares = lax.psum(jnp.sum(rows * rows, axis=1, keepdims=True), "tp")
    normed = (rows * lax.rsqrt(squares / D + 1e-05) * enc_gain.astype(jnp.float32)).astype(
        jnp.bfloat16
    )
    parts = normed.reshape((3, per_group, normed.shape[1]))
    slots = jnp.concatenate([jnp.zeros_like(parts[:1]), parts], axis=0)
    mine = lax.all_to_all(slots, "grp", split_axis=0, concat_axis=0, tiled=True)[0]
    total = jnp.dot(
        mine,
        lax.all_gather(key_value_w, "fsdp", axis=0, tiled=True),
        preferred_element_type=jnp.float32,
    )
    heads = lax.psum_scatter(
        total.reshape(per_group, heads_kv, 2 * HD), "tp", scatter_dimension=1, tiled=True
    )
    return attend_any(heads.astype(jnp.bfloat16), tiles, queries, group)


def call(body, outs, *args, specs=None, out_spec=VMEM, cost=None, scratch=()):
    outs = [jax.ShapeDtypeStruct(s, d) for s, d in outs]
    if cost is not None:
        cost = pl.CostEstimate(flops=cost * 10**9, bytes_accessed=0, transcendentals=0)
    return pl.pallas_call(
        body,
        out_shape=outs,
        in_specs=specs or [VMEM] * len(args),
        out_specs=[out_spec] * len(outs),
        cost_estimate=cost,
        scratch_shapes=list(scratch),
        compiler_params=pltpu.CompilerParams(vmem_limit_bytes=LIMIT),
    )(*args)


def join(kept, other, out):
    rows = kept.shape[0]
    out[:rows, :] = kept[...]
    out[rows:, :] = other[...]


def join_later(kept, other, after, out):
    del after
    join(kept, other, out)


def row_squares(x, after, squares):
    del after

    @pl.when(lax.axis_index("grp") == 0)
    def _():
        total = None
        for col in range(0, x.shape[1], 128):
            part = x[:, col : col + 128].astype(jnp.float32)
            total = part * part if total is None else total + part * part
        squares[...] = total


def normalise(x, squares, other, gain, a, b, c, d_low, d_high):
    width = x.shape[1] // 16

    @pl.when(lax.axis_index("grp") == 0)
    def _():
        total = jnp.sum(squares[...] + other[...], axis=1, keepdims=True)
        scale = lax.rsqrt(total / D + 1e-05)
        for z in range(4):
            for h in range(4):
                cols = slice((z * 4 + h) * width, (z * 4 + h + 1) * width)
                y = x[:, cols].astype(jnp.float32) * scale * gain[:, cols].astype(jnp.float32)
                out, at = ((a, b, c)[h], z) if h < 3 else ((d_low, d_high)[z // 2], z % 2)
                out[at] = y.astype(jnp.bfloat16)


def later(x, *rest):
    rest[-1][...] = x[...]


def landed(a, b, c, d_low, d_high, low, high):
    g = lax.axis_index("grp")
    for who, source in ((0, a), (1, b), (2, c)):

        @pl.when(g == who)
        def _(source=source):
            low[...] = source[:2]
            high[...] = source[2:]

    @pl.when(g == 3)
    def _():
        low[...] = d_low[...]
        high[...] = d_high[...]


def add_products(rows, blocks, total):
    depth = rows[0].shape[2]
    for f in range(4):

        @pl.when(lax.axis_index("fsdp") == f)
        def _(f=f):
            out = None
            for k, w in blocks.items():
                z = f ^ k
                for core in range(2):
                    y = jnp.dot(
                        rows[2 * core + z // 2][z % 2],
                        w[core * depth : (core + 1) * depth, :],
                        preferred_element_type=jnp.float32,
                    )
                    out = y if out is None else out + y
            total(out)


def products(own, near, far, *refs):
    def put(x):
        refs[4][...] = x

    add_products(refs[:4], {0: own, 1: near, 2: far}, put)


def last_product(last, *refs):
    rows, (total, mine, one, two, other, held) = refs[:4], refs[4:]
    g, n = lax.axis_index("grp"), mine.shape[0]

    def put(x):
        held[...] = total[...] + x

    add_products(rows, {3: last}, put)
    for k, out in enumerate((mine, one, two, other)):
        at = pl.multiple_of(jnp.maximum((g ^ k) - 1, 0) * n, n)
        out[...] = held[pl.ds(at, n), :].astype(out.dtype)


def attention(counts, mine, one, two, three, q_ref, out_ref, held, sems):
    g = lax.axis_index("grp")
    groups_q = QH // KVH
    copies = [
        pltpu.make_async_copy(held.at[at, :], out_ref.at[at, :], sems.at[s])
        for s, at in enumerate(pl.ds(s * TXT_S, TXT_S) for s in range(SAMP))
    ]

    @pl.when(g == 0)
    def _():
        held[...] = jnp.zeros_like(held)
        for copy in copies:
            copy.start()

    @pl.when(g > 0)
    def _():
        kv = mine[...]
        for part in (one, two, three):
            kv = kv + part[...].astype(jnp.float32)
        kv = kv.astype(jnp.bfloat16)
        slot = lax.broadcasted_iota(jnp.int32, (CAP, 1), 0)
        for s, copy in enumerate(copies):
            live = slot < counts[s : s + 1, :1]
            rows = slice(s * TXT_S, s * TXT_S + TXT_S)
            for k in range(kv.shape[1] // (2 * HD)):
                block = kv[s * CAP : s * CAP + CAP, k * 2 * HD : (k + 1) * 2 * HD]
                heads = [
                    slice((k * groups_q + j) * HD, (k * groups_q + j + 1) * HD)
                    for j in range(groups_q)
                ]
                query = jnp.concatenate([q_ref[rows, h] for h in heads], axis=0)
                scores = lax.dot_general(
                    block[:, :HD],
                    query,
                    (((1,), (1,)), ((), ())),
                    preferred_element_type=jnp.float32,
                ) * (1.0 / HD**0.5)
                scores = jnp.where(live, scores, -1e30)
                expo = jnp.exp(scores - jnp.max(scores, axis=0, keepdims=True))
                weights = (expo / jnp.sum(expo, axis=0, keepdims=True)).astype(jnp.bfloat16)
                out = lax.dot_general(
                    weights,
                    block[:, HD:],
                    (((0,), (0,)), ((), ())),
                    preferred_element_type=jnp.float32,
                )
                for j, h in enumerate(heads):
                    held[rows, h] = out[j * TXT_S : (j + 1) * TXT_S].astype(jnp.bfloat16)
            copy.start()

    for copy in copies:
        copy.wait()


def shards_line(image_rows, enc_gain, key_value_w, tiles, queries):
    g, t = lax.axis_index("grp"), lax.axis_index("tp")
    n_rows = image_rows.shape[0]
    per_group = n_rows // 3
    half = key_value_w.shape[1] // 2
    quarter = key_value_w.shape[0] // 4
    bf16, f32 = jnp.bfloat16, jnp.float32
    planes = range(4)

    def send(x, pairs):
        index = lambda p, c: (p[0] * 4 + p[1]) * 2 + c
        return lax.ppermute(x, AXES, [(index(a, c), index(b, c)) for a, b in pairs for c in (0, 1)])

    def swap(x):
        return lax.ppermute(x, "tp", [(0, 1), (1, 0)])

    w = lax.dynamic_slice_in_dim(key_value_w, g * quarter, quarter, axis=0)
    kept = lax.dynamic_slice_in_dim(w, t * half, half, axis=1)
    given = lax.dynamic_slice_in_dim(w, (1 - t) * half, half, axis=1)
    shape = (2 * quarter, half)
    other = swap(given)
    own = call(join, [(shape, bf16)], kept, other, cost=1)[0]

    def swap_planes(x, k):
        return send(x, [((c, z), (c, z ^ k)) for c in range(4) for z in planes])

    near, far, other_far = swap_planes(own, 1), swap_planes(kept, 2), swap_planes(other, 2)
    far = call(later, [(kept.shape, bf16)], far, kept, specs=[VMEM, ANY], cost=EARLY)[0]

    squares = call(row_squares, [((n_rows, 128), f32)], image_rows, own, specs=[VMEM, ANY])[0]
    whole, part = ((4, n_rows, quarter), bf16), ((2, n_rows, quarter), bf16)
    a, b, c, d_low, d_high = call(
        normalise,
        [whole] * 3 + [part] * 2,
        image_rows,
        squares,
        swap(squares),
        enc_gain.reshape(1, -1),
    )
    to_b, to_c, to_d = ([((0, z), (h, z)) for z in planes] for h in (1, 2, 3))
    d_high, b = send(d_high, to_c), send(b, to_b)
    c = call(later, [whole], c, far, specs=[VMEM, ANY], cost=0)[0]
    d_low = call(later, [part], d_low, b, specs=[VMEM, ANY], cost=0)[0]
    c, d_low = send(c, to_c), send(d_low, to_d)
    specs = [VMEM, VMEM, ANY]
    far = call(join_later, [(shape, bf16)], far, other_far, near, specs=specs, cost=COST)[0]
    last = swap_planes(far, 1)
    d_high = send(d_high, [((2, z), (3, z)) for z in planes])
    rows = call(landed, [part] * 2, a, b, c, d_low, d_high)
    rows = (*rows, *[swap(x) for x in rows])

    total = call(products, [((n_rows, half), f32)], own, near, far, *rows)[0]
    counts = lax.dynamic_slice_in_dim(tiles, jnp.maximum(g - 1, 0) * SAMP, SAMP) * TILE_TOK
    message = (per_group, half)
    mine, *parts = call(
        last_product,
        [(message, f32)] + [(message, bf16)] * 3,
        last,
        *rows,
        total,
        scratch=[pltpu.VMEM((n_rows, half), f32)],
    )
    parts = [
        send(x, [((c, z), (c ^ k, z)) for c in range(4) for z in planes])
        for k, x in zip((3, 1, 2), (parts[2], parts[0], parts[1]))
    ]
    return call(
        attention,
        [(queries.shape, bf16)],
        jnp.broadcast_to(counts[:, None], (SAMP, 128)),
        mine,
        *parts,
        queries,
        out_spec=ANY,
        scratch=[pltpu.VMEM(queries.shape, bf16), pltpu.SemaphoreType.DMA((SAMP,))],
    )[0]


def solution(mesh):
    sizes = tuple(mesh.shape[a] for a in AXES)
    return jax.shard_map(
        shards_line if sizes == (4, 4, 2) else shards_any,
        mesh=mesh,
        in_specs=(
            P(("grp", "fsdp"), "tp"),
            P("tp"),
            P(("tp", "fsdp"), None),
            P("fsdp"),
            P(("grp", "fsdp"), "tp"),
        ),
        out_specs=P(("grp", "fsdp"), "tp"),
        check_vma=False,
    )
```

```python
import jax
import jax.numpy as jnp
from jax import lax
from jax.experimental import pallas as pl
from jax.experimental.pallas import tpu as pltpu
from jax.sharding import PartitionSpec as P

D = 8192
HD = 128
KVH = 4
QH = 32
TILE_TOK = 16
SAMP = 2
TXT_S = 128
CAP = 64
AXES = ("grp", "fsdp", "tp")
VMEM = pl.BlockSpec(memory_space=pltpu.VMEM)
ANY = pl.BlockSpec(memory_space=pl.ANY)
HBM = pl.BlockSpec(memory_space=pltpu.HBM)
LIMIT = 16 * 1024 * 1024
COST = 10
EARLY = 10


def attend_any(kv, tiles, queries, group):
    local_kv = kv.shape[1]
    groups_q = QH // KVH
    kv = kv.reshape(SAMP, CAP, local_kv, 2 * HD)
    keys = kv[..., :HD]
    values = kv[..., HD:]
    query = queries.reshape(SAMP, TXT_S, local_kv, groups_q, HD)
    counts = lax.dynamic_slice_in_dim(tiles, jnp.maximum(group - 1, 0) * SAMP, SAMP) * TILE_TOK
    live = jnp.arange(CAP)[None, :] < counts[:, None]
    scores = jnp.einsum("sikgd,sjkd->skgij", query, keys, preferred_element_type=jnp.float32) * (
        1.0 / HD**0.5
    )
    scores = jnp.where(live[:, None, None, None, :], scores, -1e30)
    top = jnp.max(scores, axis=-1, keepdims=True)
    expo = jnp.exp(scores - top)
    weights = (expo / jnp.sum(expo, axis=-1, keepdims=True)).astype(jnp.bfloat16)
    out = jnp.einsum(
        "skgij,sjkd->sikgd", weights, values, preferred_element_type=jnp.float32
    ).astype(jnp.bfloat16)
    out = jnp.where(group > 0, out, jnp.zeros_like(out))
    return out.reshape(queries.shape[0], queries.shape[1])


def shards_any(image_rows, enc_gain, key_value_w, tiles, queries):
    group = lax.axis_index("grp")
    per_group = image_rows.shape[0] // 3
    heads_kv = key_value_w.shape[1] // (2 * HD)
    rows = image_rows.astype(jnp.float32)
    squares = lax.psum(jnp.sum(rows * rows, axis=1, keepdims=True), "tp")
    normed = (rows * lax.rsqrt(squares / D + 1e-05) * enc_gain.astype(jnp.float32)).astype(
        jnp.bfloat16
    )
    parts = normed.reshape((3, per_group, normed.shape[1]))
    slots = jnp.concatenate([jnp.zeros_like(parts[:1]), parts], axis=0)
    mine = lax.all_to_all(slots, "grp", split_axis=0, concat_axis=0, tiled=True)[0]
    total = jnp.dot(
        mine,
        lax.all_gather(key_value_w, "fsdp", axis=0, tiled=True),
        preferred_element_type=jnp.float32,
    )
    heads = lax.psum_scatter(
        total.reshape(per_group, heads_kv, 2 * HD), "tp", scatter_dimension=1, tiled=True
    )
    return attend_any(heads.astype(jnp.bfloat16), tiles, queries, group)


def call(body, outs, *args, specs=None, out_spec=VMEM, cost=None, scratch=(), aliases=()):
    outs = [jax.ShapeDtypeStruct(s, d) for s, d in outs]
    if cost is not None:
        cost = pl.CostEstimate(flops=cost * 10**9, bytes_accessed=0, transcendentals=0)
    return pl.pallas_call(
        body,
        out_shape=outs,
        in_specs=specs or [VMEM] * len(args),
        out_specs=out_spec if isinstance(out_spec, list) else [out_spec] * len(outs),
        cost_estimate=cost,
        scratch_shapes=list(scratch),
        input_output_aliases=dict(aliases),
        compiler_params=pltpu.CompilerParams(vmem_limit_bytes=LIMIT),
    )(*args)


def join(kept, other, out):
    rows = kept.shape[0]
    out[:rows, :] = kept[...]
    out[rows:, :] = other[...]


def join_later(kept, other, *rest):
    join(kept, other, rest[-1])


def row_squares(x, after, squares):
    del after

    @pl.when(lax.axis_index("grp") == 0)
    def _():
        total = None
        for col in range(0, x.shape[1], 128):
            part = x[:, col : col + 128].astype(jnp.float32)
            total = part * part if total is None else total + part * part
        squares[...] = total


def normalise(x, squares, other, gain, a, b, c, d_low, d_high):
    width = x.shape[1] // 16

    @pl.when(lax.axis_index("grp") == 0)
    def _():
        total = jnp.sum(squares[...] + other[...], axis=1, keepdims=True)
        scale = lax.rsqrt(total / D + 1e-05)
        for z in range(4):
            for h in range(4):
                cols = slice((z * 4 + h) * width, (z * 4 + h + 1) * width)
                y = x[:, cols].astype(jnp.float32) * scale * gain[:, cols].astype(jnp.float32)
                out, at = ((a, b, c)[h], z) if h < 3 else ((d_low, d_high)[z // 2], z % 2)
                out[at] = y.astype(jnp.bfloat16)


def later(x, *rest):
    rest[-1][...] = x[...]


def landed(a, b, c, d_low, d_high, low, high):
    g = lax.axis_index("grp")
    for who, source in ((0, a), (1, b), (2, c)):

        @pl.when(g == who)
        def _(source=source):
            low[...] = source[:2]
            high[...] = source[2:]

    @pl.when(g == 3)
    def _():
        low[...] = d_low[...]
        high[...] = d_high[...]


def add_products(rows, blocks, cores, put):
    depth = rows[0].shape[2]
    for f in range(4):

        @pl.when(lax.axis_index("fsdp") == f)
        def _(f=f):
            out = None
            for k, w in blocks.items():
                z = f ^ k
                for i, core in enumerate(cores):
                    y = jnp.dot(
                        rows[2 * i + z // 2][z % 2],
                        w[core * depth : (core + 1) * depth, :],
                        preferred_element_type=jnp.float32,
                    )
                    out = y if out is None else out + y
            put(out)


def own_products(own, near, far, low, high, total):
    def put(x):
        total[...] = x

    add_products((low, high), {0: own, 1: near, 2: far}, (0,), put)


def other_products(own, near, far, low, high, before, total):
    def put(x):
        total[...] = before[...] + x

    add_products((low, high), {0: own, 1: near, 2: far}, (1,), put)


def last_product(last, *refs):
    rows, (total, mine, one, two, other, held) = refs[:4], refs[4:]
    g, n = lax.axis_index("grp"), mine.shape[0]

    def put(x):
        held[...] = total[...] + x

    add_products(rows, {3: last}, (0, 1), put)
    for k, out in enumerate((mine, one, two, other)):
        at = pl.multiple_of(jnp.maximum((g ^ k) - 1, 0) * n, n)
        out[...] = held[pl.ds(at, n), :].astype(out.dtype)


def blank(after, out, token, held, sem):
    del after
    token[...] = jnp.zeros_like(token)

    @pl.when(lax.axis_index("grp") == 0)
    def _():
        held[...] = jnp.zeros_like(held)
        copy = pltpu.make_async_copy(held, out, sem)
        copy.start()
        copy.wait()


def attention(counts, mine, one, two, three, q_ref, blank_ref, out_ref, held, sems):
    del blank_ref
    g = lax.axis_index("grp")
    groups_q = QH // KVH
    copies = [
        pltpu.make_async_copy(held.at[at, :], out_ref.at[at, :], sems.at[s])
        for s, at in enumerate(pl.ds(s * TXT_S, TXT_S) for s in range(SAMP))
    ]

    @pl.when(g > 0)
    def _():
        kv = mine[...]
        for part in (one, two, three):
            kv = kv + part[...].astype(jnp.float32)
        kv = kv.astype(jnp.bfloat16)
        slot = lax.broadcasted_iota(jnp.int32, (CAP, 1), 0)
        for s, copy in enumerate(copies):
            live = slot < counts[s : s + 1, :1]
            rows = slice(s * TXT_S, s * TXT_S + TXT_S)
            for k in range(kv.shape[1] // (2 * HD)):
                block = kv[s * CAP : s * CAP + CAP, k * 2 * HD : (k + 1) * 2 * HD]
                heads = [
                    slice((k * groups_q + j) * HD, (k * groups_q + j + 1) * HD)
                    for j in range(groups_q)
                ]
                query = jnp.concatenate([q_ref[rows, h] for h in heads], axis=0)
                scores = lax.dot_general(
                    block[:, :HD],
                    query,
                    (((1,), (1,)), ((), ())),
                    preferred_element_type=jnp.float32,
                ) * (1.0 / HD**0.5)
                scores = jnp.where(live, scores, -1e30)
                expo = jnp.exp(scores - jnp.max(scores, axis=0, keepdims=True))
                weights = (expo / jnp.sum(expo, axis=0, keepdims=True)).astype(jnp.bfloat16)
                out = lax.dot_general(
                    weights,
                    block[:, HD:],
                    (((0,), (0,)), ((), ())),
                    preferred_element_type=jnp.float32,
                )
                for j, h in enumerate(heads):
                    held[rows, h] = out[j * TXT_S : (j + 1) * TXT_S].astype(jnp.bfloat16)
            copy.start()
        for copy in copies:
            copy.wait()


def shards_line(image_rows, enc_gain, key_value_w, tiles, queries):
    g, t = lax.axis_index("grp"), lax.axis_index("tp")
    n_rows = image_rows.shape[0]
    per_group = n_rows // 3
    half = key_value_w.shape[1] // 2
    quarter = key_value_w.shape[0] // 4
    bf16, f32 = jnp.bfloat16, jnp.float32
    planes = range(4)

    def send(x, pairs):
        index = lambda p, c: (p[0] * 4 + p[1]) * 2 + c
        return lax.ppermute(x, AXES, [(index(a, c), index(b, c)) for a, b in pairs for c in (0, 1)])

    def swap(x):
        return lax.ppermute(x, "tp", [(0, 1), (1, 0)])

    w = lax.dynamic_slice_in_dim(key_value_w, g * quarter, quarter, axis=0)
    kept = lax.dynamic_slice_in_dim(w, t * half, half, axis=1)
    given = lax.dynamic_slice_in_dim(w, (1 - t) * half, half, axis=1)
    shape = (2 * quarter, half)
    other = swap(given)
    own = call(join, [(shape, bf16)], kept, other, cost=1)[0]

    def swap_planes(x, k):
        return send(x, [((c, z), (c, z ^ k)) for c in range(4) for z in planes])

    near, far, other_far = swap_planes(own, 1), swap_planes(kept, 2), swap_planes(other, 2)
    far = call(later, [(kept.shape, bf16)], far, kept, specs=[VMEM, ANY], cost=EARLY)[0]

    squares = call(row_squares, [((n_rows, 128), f32)], image_rows, own, specs=[VMEM, ANY])[0]
    whole, part = ((4, n_rows, quarter), bf16), ((2, n_rows, quarter), bf16)
    a, b, c, d_low, d_high = call(
        normalise,
        [whole] * 3 + [part] * 2,
        image_rows,
        squares,
        swap(squares),
        enc_gain.reshape(1, -1),
    )
    to_b, to_c, to_d = ([((0, z), (h, z)) for z in planes] for h in (1, 2, 3))
    d_high, b = send(d_high, to_c), send(b, to_b)
    c = call(later, [whole], c, far, specs=[VMEM, ANY], cost=0)[0]
    d_low = call(later, [part], d_low, b, specs=[VMEM, ANY], cost=0)[0]
    c, d_low = send(c, to_c), send(d_low, to_d)
    zeros, token = call(
        blank,
        [(queries.shape, bf16), ((8, 128), f32)],
        d_high,
        out_spec=[ANY, VMEM],
        specs=[ANY],
        cost=0,
        scratch=[pltpu.VMEM(queries.shape, bf16), pltpu.SemaphoreType.DMA],
    )
    specs = [VMEM, VMEM, ANY, ANY]
    far = call(join_later, [(shape, bf16)], far, other_far, near, token, specs=specs, cost=COST)[0]
    last = swap_planes(far, 1)
    d_high = send(d_high, [((2, z), (3, z)) for z in planes])
    rows = call(landed, [part] * 2, a, b, c, d_low, d_high)
    others = [swap(x) for x in rows]

    total, blocks = [((n_rows, half), f32)], (own, near, far)
    before = call(own_products, total, *blocks, *rows, cost=0)[0]
    total = call(other_products, total, *blocks, *others, before, cost=0)[0]
    counts = lax.dynamic_slice_in_dim(tiles, jnp.maximum(g - 1, 0) * SAMP, SAMP) * TILE_TOK
    message = (per_group, half)
    mine, *parts = call(
        last_product,
        [(message, f32)] + [(message, bf16)] * 3,
        last,
        *rows,
        *others,
        total,
        scratch=[pltpu.VMEM((n_rows, half), f32)],
    )
    parts = [
        send(x, [((c, z), (c ^ k, z)) for c in range(4) for z in planes])
        for k, x in zip((3, 1, 2), (parts[2], parts[0], parts[1]))
    ]
    return call(
        attention,
        [(queries.shape, bf16)],
        jnp.broadcast_to(counts[:, None], (SAMP, 128)),
        mine,
        *parts,
        queries,
        zeros,
        specs=[VMEM] * 6 + [ANY],
        out_spec=ANY,
        aliases={6: 0},
        scratch=[pltpu.VMEM(queries.shape, bf16), pltpu.SemaphoreType.DMA((SAMP,))],
    )[0]


def solution(mesh):
    sizes = tuple(mesh.shape[a] for a in AXES)
    return jax.shard_map(
        shards_line if sizes == (4, 4, 2) else shards_any,
        mesh=mesh,
        in_specs=(
            P(("grp", "fsdp"), "tp"),
            P("tp"),
            P(("tp", "fsdp"), None),
            P("fsdp"),
            P(("grp", "fsdp"), "tp"),
        ),
        out_specs=P(("grp", "fsdp"), "tp"),
        check_vma=False,
    )
```

```python
import jax
import jax.numpy as jnp
from jax import lax
from jax.experimental import pallas as pl
from jax.experimental.pallas import tpu as pltpu
from jax.sharding import PartitionSpec as P

D = 8192
HD = 128
KVH = 4
QH = 32
TILE_TOK = 16
SAMP = 2
TXT_S = 128
CAP = 64
AXES = ("grp", "fsdp", "tp")
VMEM = pl.BlockSpec(memory_space=pltpu.VMEM)
ANY = pl.BlockSpec(memory_space=pl.ANY)
HBM = pl.BlockSpec(memory_space=pltpu.HBM)
LIMIT = 16 * 1024 * 1024
COST = 10
EARLY = 10


def attend_any(kv, tiles, queries, group):
    local_kv = kv.shape[1]
    groups_q = QH // KVH
    kv = kv.reshape(SAMP, CAP, local_kv, 2 * HD)
    keys = kv[..., :HD]
    values = kv[..., HD:]
    query = queries.reshape(SAMP, TXT_S, local_kv, groups_q, HD)
    counts = lax.dynamic_slice_in_dim(tiles, jnp.maximum(group - 1, 0) * SAMP, SAMP) * TILE_TOK
    live = jnp.arange(CAP)[None, :] < counts[:, None]
    scores = jnp.einsum("sikgd,sjkd->skgij", query, keys, preferred_element_type=jnp.float32) * (
        1.0 / HD**0.5
    )
    scores = jnp.where(live[:, None, None, None, :], scores, -1e30)
    top = jnp.max(scores, axis=-1, keepdims=True)
    expo = jnp.exp(scores - top)
    weights = (expo / jnp.sum(expo, axis=-1, keepdims=True)).astype(jnp.bfloat16)
    out = jnp.einsum(
        "skgij,sjkd->sikgd", weights, values, preferred_element_type=jnp.float32
    ).astype(jnp.bfloat16)
    out = jnp.where(group > 0, out, jnp.zeros_like(out))
    return out.reshape(queries.shape[0], queries.shape[1])


def shards_any(image_rows, enc_gain, key_value_w, tiles, queries):
    group = lax.axis_index("grp")
    per_group = image_rows.shape[0] // 3
    heads_kv = key_value_w.shape[1] // (2 * HD)
    rows = image_rows.astype(jnp.float32)
    squares = lax.psum(jnp.sum(rows * rows, axis=1, keepdims=True), "tp")
    normed = (rows * lax.rsqrt(squares / D + 1e-05) * enc_gain.astype(jnp.float32)).astype(
        jnp.bfloat16
    )
    parts = normed.reshape((3, per_group, normed.shape[1]))
    slots = jnp.concatenate([jnp.zeros_like(parts[:1]), parts], axis=0)
    mine = lax.all_to_all(slots, "grp", split_axis=0, concat_axis=0, tiled=True)[0]
    total = jnp.dot(
        mine,
        lax.all_gather(key_value_w, "fsdp", axis=0, tiled=True),
        preferred_element_type=jnp.float32,
    )
    heads = lax.psum_scatter(
        total.reshape(per_group, heads_kv, 2 * HD), "tp", scatter_dimension=1, tiled=True
    )
    return attend_any(heads.astype(jnp.bfloat16), tiles, queries, group)


def call(body, outs, *args, specs=None, out_spec=VMEM, cost=None, scratch=(), aliases=()):
    outs = [jax.ShapeDtypeStruct(s, d) for s, d in outs]
    if cost is not None:
        cost = pl.CostEstimate(flops=cost * 10**9, bytes_accessed=0, transcendentals=0)
    return pl.pallas_call(
        body,
        out_shape=outs,
        in_specs=specs or [VMEM] * len(args),
        out_specs=out_spec if isinstance(out_spec, list) else [out_spec] * len(outs),
        cost_estimate=cost,
        scratch_shapes=list(scratch),
        input_output_aliases=dict(aliases),
        compiler_params=pltpu.CompilerParams(vmem_limit_bytes=LIMIT),
    )(*args)


def join(kept, other, out):
    rows = kept.shape[0]
    out[:rows, :] = kept[...]
    out[rows:, :] = other[...]


def join_later(kept, other, *rest):
    join(kept, other, rest[-1])


def row_squares(x, after, squares):
    del after

    @pl.when(lax.axis_index("grp") == 0)
    def _():
        total = None
        for col in range(0, x.shape[1], 128):
            part = x[:, col : col + 128].astype(jnp.float32)
            total = part * part if total is None else total + part * part
        squares[...] = total


def normalise(x, squares, other, gain, a, b, c, d_low, d_high):
    width = x.shape[1] // 16

    @pl.when(lax.axis_index("grp") == 0)
    def _():
        total = jnp.sum(squares[...] + other[...], axis=1, keepdims=True)
        scale = lax.rsqrt(total / D + 1e-05)
        for z in range(4):
            for h in range(4):
                cols = slice((z * 4 + h) * width, (z * 4 + h + 1) * width)
                y = x[:, cols].astype(jnp.float32) * scale * gain[:, cols].astype(jnp.float32)
                out, at = ((a, b, c)[h], z) if h < 3 else ((d_low, d_high)[z // 2], z % 2)
                out[at] = y.astype(jnp.bfloat16)


def later(x, *rest):
    rest[-1][...] = x[...]


def landed(a, b, c, d_low, d_high, low, high):
    g = lax.axis_index("grp")
    for who, source in ((0, a), (1, b), (2, c)):

        @pl.when(g == who)
        def _(source=source):
            low[...] = source[:2]
            high[...] = source[2:]

    @pl.when(g == 3)
    def _():
        low[...] = d_low[...]
        high[...] = d_high[...]


def add_products(rows, blocks, cores, put):
    depth = rows[0].shape[2]
    for f in range(4):

        @pl.when(lax.axis_index("fsdp") == f)
        def _(f=f):
            out = None
            for k, w in blocks.items():
                z = f ^ k
                for i, core in enumerate(cores):
                    y = jnp.dot(
                        rows[2 * i + z // 2][z % 2],
                        w[core * depth : (core + 1) * depth, :],
                        preferred_element_type=jnp.float32,
                    )
                    out = y if out is None else out + y
            put(out)


def own_products(own, near, far, low, high, total):
    def put(x):
        total[...] = x

    add_products((low, high), {0: own, 1: near, 2: far}, (0,), put)


def other_products(own, near, far, low, high, before, total):
    def put(x):
        total[...] = before[...] + x

    add_products((low, high), {0: own, 1: near, 2: far}, (1,), put)


def last_product(last, *refs):
    rows, (total, mine, one, two, other, held) = refs[:4], refs[4:]
    g, n = lax.axis_index("grp"), mine.shape[0]

    def put(x):
        held[...] = total[...] + x

    add_products(rows, {3: last}, (0, 1), put)
    for k, out in enumerate((mine, one, two, other)):
        at = pl.multiple_of(jnp.maximum((g ^ k) - 1, 0) * n, n)
        out[...] = held[pl.ds(at, n), :].astype(out.dtype)


def blank(after, out, token, held, sem):
    del after
    token[...] = jnp.zeros_like(token)

    @pl.when(lax.axis_index("grp") == 0)
    def _():
        held[...] = jnp.zeros_like(held)
        copy = pltpu.make_async_copy(held, out, sem)
        copy.start()
        copy.wait()


def attention(counts, mine, one, two, three, q_ref, blank_ref, out_ref, held, sems):
    del blank_ref
    g = lax.axis_index("grp")
    groups_q = QH // KVH
    copies = [
        pltpu.make_async_copy(held.at[at, :], out_ref.at[at, :], sems.at[s])
        for s, at in enumerate(pl.ds(s * TXT_S, TXT_S) for s in range(SAMP))
    ]

    @pl.when(g > 0)
    def _():
        kv = mine[...]
        for part in (one, two, three):
            kv = kv + part[...].astype(jnp.float32)
        kv = kv.astype(jnp.bfloat16)
        slot = lax.broadcasted_iota(jnp.int32, (CAP, 1), 0)
        width = 2 * HD
        pairs = [(s, k) for s in range(SAMP) for k in range(kv.shape[1] // width)]
        block = {
            (s, k): kv[s * CAP : s * CAP + CAP, k * width : (k + 1) * width] for s, k in pairs
        }
        rows = [slice(s * TXT_S, s * TXT_S + TXT_S) for s in range(SAMP)]

        def heads(k):
            return [slice(h * HD, (h + 1) * HD) for h in range(k * groups_q, (k + 1) * groups_q)]

        scores = {}
        for s, k in pairs:
            query = jnp.concatenate([q_ref[rows[s], h] for h in heads(k)], axis=0)
            scores[s, k] = lax.dot_general(
                block[s, k][:, :HD],
                query,
                (((1,), (1,)), ((), ())),
                preferred_element_type=jnp.float32,
            ) * (1.0 / HD**0.5)
        for s, copy in enumerate(copies):
            live = slot < counts[s : s + 1, :1]
            weights = {}
            for k in [k for r, k in pairs if r == s]:
                x = jnp.where(live, scores[s, k], -1e30)
                expo = jnp.exp(x - jnp.max(x, axis=0, keepdims=True))
                weights[k] = (expo / jnp.sum(expo, axis=0, keepdims=True)).astype(jnp.bfloat16)
            for k, w in weights.items():
                out = lax.dot_general(
                    w,
                    block[s, k][:, HD:],
                    (((0,), (0,)), ((), ())),
                    preferred_element_type=jnp.float32,
                )
                for j, h in enumerate(heads(k)):
                    held[rows[s], h] = out[j * TXT_S : (j + 1) * TXT_S].astype(jnp.bfloat16)
            copy.start()
        for copy in copies:
            copy.wait()


def shards_line(image_rows, enc_gain, key_value_w, tiles, queries):
    g, t = lax.axis_index("grp"), lax.axis_index("tp")
    n_rows = image_rows.shape[0]
    per_group = n_rows // 3
    half = key_value_w.shape[1] // 2
    quarter = key_value_w.shape[0] // 4
    bf16, f32 = jnp.bfloat16, jnp.float32
    planes = range(4)

    def send(x, pairs):
        index = lambda p, c: (p[0] * 4 + p[1]) * 2 + c
        return lax.ppermute(x, AXES, [(index(a, c), index(b, c)) for a, b in pairs for c in (0, 1)])

    def swap(x):
        return lax.ppermute(x, "tp", [(0, 1), (1, 0)])

    w = lax.dynamic_slice_in_dim(key_value_w, g * quarter, quarter, axis=0)
    kept = lax.dynamic_slice_in_dim(w, t * half, half, axis=1)
    given = lax.dynamic_slice_in_dim(w, (1 - t) * half, half, axis=1)
    shape = (2 * quarter, half)
    other = swap(given)
    own = call(join, [(shape, bf16)], kept, other, cost=1)[0]

    def swap_planes(x, k):
        return send(x, [((c, z), (c, z ^ k)) for c in range(4) for z in planes])

    near, far, other_far = swap_planes(own, 1), swap_planes(kept, 2), swap_planes(other, 2)
    far = call(later, [(kept.shape, bf16)], far, kept, specs=[VMEM, ANY], cost=EARLY)[0]

    squares = call(row_squares, [((n_rows, 128), f32)], image_rows, own, specs=[VMEM, ANY])[0]
    whole, part = ((4, n_rows, quarter), bf16), ((2, n_rows, quarter), bf16)
    a, b, c, d_low, d_high = call(
        normalise,
        [whole] * 3 + [part] * 2,
        image_rows,
        squares,
        swap(squares),
        enc_gain.reshape(1, -1),
    )
    to_b, to_c, to_d = ([((0, z), (h, z)) for z in planes] for h in (1, 2, 3))
    d_high, b = send(d_high, to_c), send(b, to_b)
    c = call(later, [whole], c, far, specs=[VMEM, ANY], cost=0)[0]
    d_low = call(later, [part], d_low, b, specs=[VMEM, ANY], cost=0)[0]
    c, d_low = send(c, to_c), send(d_low, to_d)
    zeros, token = call(
        blank,
        [(queries.shape, bf16), ((8, 128), f32)],
        d_high,
        out_spec=[ANY, VMEM],
        specs=[ANY],
        cost=0,
        scratch=[pltpu.VMEM(queries.shape, bf16), pltpu.SemaphoreType.DMA],
    )
    specs = [VMEM, VMEM, ANY, ANY]
    far = call(join_later, [(shape, bf16)], far, other_far, near, token, specs=specs, cost=COST)[0]
    last = swap_planes(far, 1)
    d_high = send(d_high, [((2, z), (3, z)) for z in planes])
    rows = call(landed, [part] * 2, a, b, c, d_low, d_high)
    others = [swap(x) for x in rows]

    total, blocks = [((n_rows, half), f32)], (own, near, far)
    before = call(own_products, total, *blocks, *rows, cost=0)[0]
    total = call(other_products, total, *blocks, *others, before, cost=0)[0]
    counts = lax.dynamic_slice_in_dim(tiles, jnp.maximum(g - 1, 0) * SAMP, SAMP) * TILE_TOK
    message = (per_group, half)
    mine, *parts = call(
        last_product,
        [(message, f32)] + [(message, bf16)] * 3,
        last,
        *rows,
        *others,
        total,
        scratch=[pltpu.VMEM((n_rows, half), f32)],
    )
    parts = [
        send(x, [((c, z), (c ^ k, z)) for c in range(4) for z in planes])
        for k, x in zip((3, 1, 2), (parts[2], parts[0], parts[1]))
    ]
    return call(
        attention,
        [(queries.shape, bf16)],
        jnp.broadcast_to(counts[:, None], (SAMP, 128)),
        mine,
        *parts,
        queries,
        zeros,
        specs=[VMEM] * 6 + [ANY],
        out_spec=ANY,
        aliases={6: 0},
        scratch=[pltpu.VMEM(queries.shape, bf16), pltpu.SemaphoreType.DMA((SAMP,))],
    )[0]


def solution(mesh):
    sizes = tuple(mesh.shape[a] for a in AXES)
    return jax.shard_map(
        shards_line if sizes == (4, 4, 2) else shards_any,
        mesh=mesh,
        in_specs=(
            P(("grp", "fsdp"), "tp"),
            P("tp"),
            P(("tp", "fsdp"), None),
            P("fsdp"),
            P(("grp", "fsdp"), "tp"),
        ),
        out_specs=P(("grp", "fsdp"), "tp"),
        check_vma=False,
    )
```

```python
import jax
import jax.numpy as jnp
from jax import lax
from jax.experimental import pallas as pl
from jax.experimental.pallas import tpu as pltpu
from jax.sharding import PartitionSpec as P

D = 8192
HD = 128
KVH = 4
QH = 32
TILE_TOK = 16
SAMP = 2
TXT_S = 128
CAP = 64
AXES = ("grp", "fsdp", "tp")
VMEM = pl.BlockSpec(memory_space=pltpu.VMEM)
ANY = pl.BlockSpec(memory_space=pl.ANY)
HBM = pl.BlockSpec(memory_space=pltpu.HBM)
LIMIT = 16 * 1024 * 1024
COST = 10
EARLY = 10


def attend_any(kv, tiles, queries, group):
    local_kv = kv.shape[1]
    groups_q = QH // KVH
    kv = kv.reshape(SAMP, CAP, local_kv, 2 * HD)
    keys = kv[..., :HD]
    values = kv[..., HD:]
    query = queries.reshape(SAMP, TXT_S, local_kv, groups_q, HD)
    counts = lax.dynamic_slice_in_dim(tiles, jnp.maximum(group - 1, 0) * SAMP, SAMP) * TILE_TOK
    live = jnp.arange(CAP)[None, :] < counts[:, None]
    scores = jnp.einsum("sikgd,sjkd->skgij", query, keys, preferred_element_type=jnp.float32) * (
        1.0 / HD**0.5
    )
    scores = jnp.where(live[:, None, None, None, :], scores, -1e30)
    top = jnp.max(scores, axis=-1, keepdims=True)
    expo = jnp.exp(scores - top)
    weights = (expo / jnp.sum(expo, axis=-1, keepdims=True)).astype(jnp.bfloat16)
    out = jnp.einsum(
        "skgij,sjkd->sikgd", weights, values, preferred_element_type=jnp.float32
    ).astype(jnp.bfloat16)
    out = jnp.where(group > 0, out, jnp.zeros_like(out))
    return out.reshape(queries.shape[0], queries.shape[1])


def shards_any(image_rows, enc_gain, key_value_w, tiles, queries):
    group = lax.axis_index("grp")
    per_group = image_rows.shape[0] // 3
    heads_kv = key_value_w.shape[1] // (2 * HD)
    rows = image_rows.astype(jnp.float32)
    squares = lax.psum(jnp.sum(rows * rows, axis=1, keepdims=True), "tp")
    normed = (rows * lax.rsqrt(squares / D + 1e-05) * enc_gain.astype(jnp.float32)).astype(
        jnp.bfloat16
    )
    parts = normed.reshape((3, per_group, normed.shape[1]))
    slots = jnp.concatenate([jnp.zeros_like(parts[:1]), parts], axis=0)
    mine = lax.all_to_all(slots, "grp", split_axis=0, concat_axis=0, tiled=True)[0]
    total = jnp.dot(
        mine,
        lax.all_gather(key_value_w, "fsdp", axis=0, tiled=True),
        preferred_element_type=jnp.float32,
    )
    heads = lax.psum_scatter(
        total.reshape(per_group, heads_kv, 2 * HD), "tp", scatter_dimension=1, tiled=True
    )
    return attend_any(heads.astype(jnp.bfloat16), tiles, queries, group)


def call(body, outs, *args, specs=None, out_spec=VMEM, cost=None, scratch=(), aliases=()):
    outs = [jax.ShapeDtypeStruct(s, d) for s, d in outs]
    if cost is not None:
        cost = pl.CostEstimate(flops=cost * 10**9, bytes_accessed=0, transcendentals=0)
    return pl.pallas_call(
        body,
        out_shape=outs,
        in_specs=specs or [VMEM] * len(args),
        out_specs=out_spec if isinstance(out_spec, list) else [out_spec] * len(outs),
        cost_estimate=cost,
        scratch_shapes=list(scratch),
        input_output_aliases=dict(aliases),
        compiler_params=pltpu.CompilerParams(vmem_limit_bytes=LIMIT),
    )(*args)


def join(kept, other, out):
    rows = kept.shape[0]
    out[:rows, :] = kept[...]
    out[rows:, :] = other[...]


def join_later(kept, other, *rest):
    join(kept, other, rest[-1])


def row_squares(x, after, squares):
    del after

    @pl.when(lax.axis_index("grp") == 0)
    def _():
        total = None
        for col in range(0, x.shape[1], 128):
            part = x[:, col : col + 128].astype(jnp.float32)
            total = part * part if total is None else total + part * part
        squares[...] = total


def normalise(x, squares, other, gain, a, b, c, d_low, d_high):
    lanes = gain.shape[1]
    tiles = x.shape[1] // 16 // lanes

    @pl.when(lax.axis_index("grp") == 0)
    def _():
        total = jnp.sum(squares[...] + other[...], axis=1, keepdims=True)
        scale = lax.rsqrt(total / D + 1e-05)
        gains = gain[...].astype(jnp.float32)
        for z in range(4):
            for h in range(4):
                out, at = ((a, b, c)[h], z) if h < 3 else ((d_low, d_high)[z // 2], z % 2)
                for i in range(tiles):
                    k = (z * 4 + h) * tiles + i
                    y = x[:, k * lanes : (k + 1) * lanes].astype(jnp.float32) * scale
                    y = y * gains[k : k + 1]
                    out[at, :, i * lanes : (i + 1) * lanes] = y.astype(jnp.bfloat16)


def later(x, *rest):
    rest[-1][...] = x[...]


def landed(a, b, c, d_low, d_high, low, high):
    g = lax.axis_index("grp")
    for who, source in ((0, a), (1, b), (2, c)):

        @pl.when(g == who)
        def _(source=source):
            low[...] = source[:2]
            high[...] = source[2:]

    @pl.when(g == 3)
    def _():
        low[...] = d_low[...]
        high[...] = d_high[...]


def add_products(rows, blocks, cores, put):
    depth = rows[0].shape[2]
    for f in range(4):

        @pl.when(lax.axis_index("fsdp") == f)
        def _(f=f):
            out = None
            for k, w in blocks.items():
                z = f ^ k
                for i, core in enumerate(cores):
                    y = jnp.dot(
                        rows[2 * i + z // 2][z % 2],
                        w[core * depth : (core + 1) * depth, :],
                        preferred_element_type=jnp.float32,
                    )
                    out = y if out is None else out + y
            put(out)


def own_products(own, near, far, low, high, total):
    def put(x):
        total[...] = x

    add_products((low, high), {0: own, 1: near, 2: far}, (0,), put)


def other_products(own, near, far, low, high, before, total):
    def put(x):
        total[...] = before[...] + x

    add_products((low, high), {0: own, 1: near, 2: far}, (1,), put)


def last_product(last, *refs):
    rows, (total, mine, one, two, other, held) = refs[:4], refs[4:]
    g, n = lax.axis_index("grp"), mine.shape[0]

    def put(x):
        held[...] = total[...] + x

    add_products(rows, {3: last}, (0, 1), put)
    for k, out in enumerate((mine, one, two, other)):
        at = pl.multiple_of(jnp.maximum((g ^ k) - 1, 0) * n, n)
        out[...] = held[pl.ds(at, n), :].astype(out.dtype)


def blank(after, out, token, held, sem):
    del after
    token[...] = jnp.zeros_like(token)

    @pl.when(lax.axis_index("grp") == 0)
    def _():
        held[...] = jnp.zeros_like(held)
        copy = pltpu.make_async_copy(held, out, sem)
        copy.start()
        copy.wait()


def attention(counts, mine, one, two, three, q_ref, blank_ref, out_ref, held, sems):
    del blank_ref
    g = lax.axis_index("grp")
    groups_q = QH // KVH
    copies = [
        pltpu.make_async_copy(held.at[at, :], out_ref.at[at, :], sems.at[s])
        for s, at in enumerate(pl.ds(s * TXT_S, TXT_S) for s in range(SAMP))
    ]

    @pl.when(g > 0)
    def _():
        kv = mine[...]
        for part in (one, two, three):
            kv = kv + part[...].astype(jnp.float32)
        kv = kv.astype(jnp.bfloat16)
        slot = lax.broadcasted_iota(jnp.int32, (CAP, 1), 0)
        width = 2 * HD
        pairs = [(s, k) for s in range(SAMP) for k in range(kv.shape[1] // width)]
        block = {
            (s, k): kv[s * CAP : s * CAP + CAP, k * width : (k + 1) * width] for s, k in pairs
        }
        rows = [slice(s * TXT_S, s * TXT_S + TXT_S) for s in range(SAMP)]

        def heads(k):
            return [slice(h * HD, (h + 1) * HD) for h in range(k * groups_q, (k + 1) * groups_q)]

        scores = {}
        for s, k in pairs:
            query = jnp.concatenate([q_ref[rows[s], h] for h in heads(k)], axis=0)
            scores[s, k] = lax.dot_general(
                block[s, k][:, :HD],
                query,
                (((1,), (1,)), ((), ())),
                preferred_element_type=jnp.float32,
            ) * (1.0 / HD**0.5)
        for s, copy in enumerate(copies):
            live = slot < counts[s : s + 1, :1]
            weights = {}
            for k in [k for r, k in pairs if r == s]:
                x = jnp.where(live, scores[s, k], -1e30)
                expo = jnp.exp(x - jnp.max(x, axis=0, keepdims=True))
                weights[k] = (expo / jnp.sum(expo, axis=0, keepdims=True)).astype(jnp.bfloat16)
            for k, w in weights.items():
                out = lax.dot_general(
                    w,
                    block[s, k][:, HD:],
                    (((0,), (0,)), ((), ())),
                    preferred_element_type=jnp.float32,
                )
                for j, h in enumerate(heads(k)):
                    held[rows[s], h] = out[j * TXT_S : (j + 1) * TXT_S].astype(jnp.bfloat16)
            copy.start()
        for copy in copies:
            copy.wait()


def shards_line(image_rows, enc_gain, key_value_w, tiles, queries):
    g, t = lax.axis_index("grp"), lax.axis_index("tp")
    n_rows = image_rows.shape[0]
    per_group = n_rows // 3
    half = key_value_w.shape[1] // 2
    quarter = key_value_w.shape[0] // 4
    bf16, f32 = jnp.bfloat16, jnp.float32
    planes = range(4)

    def send(x, pairs):
        index = lambda p, c: (p[0] * 4 + p[1]) * 2 + c
        return lax.ppermute(x, AXES, [(index(a, c), index(b, c)) for a, b in pairs for c in (0, 1)])

    def swap(x):
        return lax.ppermute(x, "tp", [(0, 1), (1, 0)])

    w = lax.dynamic_slice_in_dim(key_value_w, g * quarter, quarter, axis=0)
    kept = lax.dynamic_slice_in_dim(w, t * half, half, axis=1)
    given = lax.dynamic_slice_in_dim(w, (1 - t) * half, half, axis=1)
    shape = (2 * quarter, half)
    other = swap(given)
    own = call(join, [(shape, bf16)], kept, other, cost=1)[0]

    def swap_planes(x, k):
        return send(x, [((c, z), (c, z ^ k)) for c in range(4) for z in planes])

    near, far = swap_planes(own, 1), swap_planes(kept, 2)
    far = call(later, [(kept.shape, bf16)], far, kept, specs=[VMEM, ANY], cost=EARLY)[0]

    squares = call(row_squares, [((n_rows, 128), f32)], image_rows, own, specs=[VMEM, ANY])[0]
    whole, part = ((4, n_rows, quarter), bf16), ((2, n_rows, quarter), bf16)
    a, b, c, d_low, d_high = call(
        normalise,
        [whole] * 3 + [part] * 2,
        image_rows,
        squares,
        swap(squares),
        enc_gain.reshape(-1, 128),
    )
    other_far = call(later, [(kept.shape, bf16)], other, a, specs=[VMEM, ANY], cost=0)[0]
    other_far = swap_planes(other_far, 2)
    to_b, to_c, to_d = ([((0, z), (h, z)) for z in planes] for h in (1, 2, 3))
    d_high, b = send(d_high, to_c), send(b, to_b)
    c = call(later, [whole], c, far, specs=[VMEM, ANY], cost=0)[0]
    d_low = call(later, [part], d_low, b, specs=[VMEM, ANY], cost=0)[0]
    c, d_low = send(c, to_c), send(d_low, to_d)
    zeros, token = call(
        blank,
        [(queries.shape, bf16), ((8, 128), f32)],
        d_high,
        out_spec=[ANY, VMEM],
        specs=[ANY],
        cost=0,
        scratch=[pltpu.VMEM(queries.shape, bf16), pltpu.SemaphoreType.DMA],
    )
    specs = [VMEM, VMEM, ANY, ANY]
    far = call(join_later, [(shape, bf16)], far, other_far, near, token, specs=specs, cost=COST)[0]
    last = swap_planes(far, 1)
    d_high = send(d_high, [((2, z), (3, z)) for z in planes])
    rows = call(landed, [part] * 2, a, b, c, d_low, d_high)
    others = [swap(x) for x in rows]

    total, blocks = [((n_rows, half), f32)], (own, near, far)
    before = call(own_products, total, *blocks, *rows, cost=0)[0]
    total = call(other_products, total, *blocks, *others, before, cost=0)[0]
    counts = lax.dynamic_slice_in_dim(tiles, jnp.maximum(g - 1, 0) * SAMP, SAMP) * TILE_TOK
    message = (per_group, half)
    mine, *parts = call(
        last_product,
        [(message, f32)] + [(message, bf16)] * 3,
        last,
        *rows,
        *others,
        total,
        scratch=[pltpu.VMEM((n_rows, half), f32)],
    )
    parts = [
        send(x, [((c, z), (c ^ k, z)) for c in range(4) for z in planes])
        for k, x in zip((3, 1, 2), (parts[2], parts[0], parts[1]))
    ]
    return call(
        attention,
        [(queries.shape, bf16)],
        jnp.broadcast_to(counts[:, None], (SAMP, 128)),
        mine,
        *parts,
        queries,
        zeros,
        specs=[VMEM] * 6 + [ANY],
        out_spec=ANY,
        aliases={6: 0},
        scratch=[pltpu.VMEM(queries.shape, bf16), pltpu.SemaphoreType.DMA((SAMP,))],
    )[0]


def solution(mesh):
    sizes = tuple(mesh.shape[a] for a in AXES)
    return jax.shard_map(
        shards_line if sizes == (4, 4, 2) else shards_any,
        mesh=mesh,
        in_specs=(
            P(("grp", "fsdp"), "tp"),
            P("tp"),
            P(("tp", "fsdp"), None),
            P("fsdp"),
            P(("grp", "fsdp"), "tp"),
        ),
        out_specs=P(("grp", "fsdp"), "tp"),
        check_vma=False,
    )
```

```python
import jax
import jax.numpy as jnp
from jax import lax
from jax.experimental import pallas as pl
from jax.experimental.pallas import tpu as pltpu
from jax.sharding import PartitionSpec as P

D = 8192
HD = 128
KVH = 4
QH = 32
TILE_TOK = 16
SAMP = 2
TXT_S = 128
CAP = 64
AXES = ("grp", "fsdp", "tp")
VMEM = pl.BlockSpec(memory_space=pltpu.VMEM)
ANY = pl.BlockSpec(memory_space=pl.ANY)
HBM = pl.BlockSpec(memory_space=pltpu.HBM)
LIMIT = 16 * 1024 * 1024
COST = 10
EARLY = 10


def attend_any(kv, tiles, queries, group):
    local_kv = kv.shape[1]
    groups_q = QH // KVH
    kv = kv.reshape(SAMP, CAP, local_kv, 2 * HD)
    keys = kv[..., :HD]
    values = kv[..., HD:]
    query = queries.reshape(SAMP, TXT_S, local_kv, groups_q, HD)
    counts = lax.dynamic_slice_in_dim(tiles, jnp.maximum(group - 1, 0) * SAMP, SAMP) * TILE_TOK
    live = jnp.arange(CAP)[None, :] < counts[:, None]
    scores = jnp.einsum("sikgd,sjkd->skgij", query, keys, preferred_element_type=jnp.float32) * (
        1.0 / HD**0.5
    )
    scores = jnp.where(live[:, None, None, None, :], scores, -1e30)
    top = jnp.max(scores, axis=-1, keepdims=True)
    expo = jnp.exp(scores - top)
    weights = (expo / jnp.sum(expo, axis=-1, keepdims=True)).astype(jnp.bfloat16)
    out = jnp.einsum(
        "skgij,sjkd->sikgd", weights, values, preferred_element_type=jnp.float32
    ).astype(jnp.bfloat16)
    out = jnp.where(group > 0, out, jnp.zeros_like(out))
    return out.reshape(queries.shape[0], queries.shape[1])


def shards_any(image_rows, enc_gain, key_value_w, tiles, queries):
    group = lax.axis_index("grp")
    per_group = image_rows.shape[0] // 3
    heads_kv = key_value_w.shape[1] // (2 * HD)
    rows = image_rows.astype(jnp.float32)
    squares = lax.psum(jnp.sum(rows * rows, axis=1, keepdims=True), "tp")
    normed = (rows * lax.rsqrt(squares / D + 1e-05) * enc_gain.astype(jnp.float32)).astype(
        jnp.bfloat16
    )
    parts = normed.reshape((3, per_group, normed.shape[1]))
    slots = jnp.concatenate([jnp.zeros_like(parts[:1]), parts], axis=0)
    mine = lax.all_to_all(slots, "grp", split_axis=0, concat_axis=0, tiled=True)[0]
    total = jnp.dot(
        mine,
        lax.all_gather(key_value_w, "fsdp", axis=0, tiled=True),
        preferred_element_type=jnp.float32,
    )
    heads = lax.psum_scatter(
        total.reshape(per_group, heads_kv, 2 * HD), "tp", scatter_dimension=1, tiled=True
    )
    return attend_any(heads.astype(jnp.bfloat16), tiles, queries, group)


def call(body, outs, *args, specs=None, out_spec=VMEM, cost=None, scratch=(), aliases=()):
    outs = [jax.ShapeDtypeStruct(s, d) for s, d in outs]
    if cost is not None:
        cost = pl.CostEstimate(flops=cost * 10**9, bytes_accessed=0, transcendentals=0)
    return pl.pallas_call(
        body,
        out_shape=outs,
        in_specs=specs or [VMEM] * len(args),
        out_specs=out_spec if isinstance(out_spec, list) else [out_spec] * len(outs),
        cost_estimate=cost,
        scratch_shapes=list(scratch),
        input_output_aliases=dict(aliases),
        compiler_params=pltpu.CompilerParams(vmem_limit_bytes=LIMIT),
    )(*args)


def join(kept, other, out):
    rows = kept.shape[0]
    out[:rows, :] = kept[...]
    out[rows:, :] = other[...]


def join_later(kept, other, *rest):
    join(kept, other, rest[-1])


def row_squares(x, after, squares):
    del after

    @pl.when(lax.axis_index("grp") == 0)
    def _():
        total = None
        for col in range(0, x.shape[1], 128):
            part = x[:, col : col + 128].astype(jnp.float32)
            total = part * part if total is None else total + part * part
        squares[...] = total


def normalise(x, squares, other, gain, a, b, c, d_low, d_high):
    lanes = gain.shape[1]
    tiles = x.shape[1] // 16 // lanes

    @pl.when(lax.axis_index("grp") == 0)
    def _():
        total = jnp.sum(squares[...] + other[...], axis=1, keepdims=True)
        scale = lax.rsqrt(total / D + 1e-05)
        gains = gain[...].astype(jnp.float32)
        for z in range(4):
            for h in range(4):
                out, at = ((a, b, c)[h], z) if h < 3 else ((d_low, d_high)[z // 2], z % 2)
                for i in range(tiles):
                    k = (z * 4 + h) * tiles + i
                    y = x[:, k * lanes : (k + 1) * lanes].astype(jnp.float32) * scale
                    y = y * gains[k : k + 1]
                    out[at, :, i * lanes : (i + 1) * lanes] = y.astype(jnp.bfloat16)


def later(x, *rest):
    rest[-1][...] = x[...]


def landed(a, b, c, d_low, d_high, low, high):
    g = lax.axis_index("grp")
    for who, source in ((0, a), (1, b), (2, c)):

        @pl.when(g == who)
        def _(source=source):
            low[...] = source[:2]
            high[...] = source[2:]

    @pl.when(g == 3)
    def _():
        low[...] = d_low[...]
        high[...] = d_high[...]


def add_products(rows, blocks, cores, put):
    depth = rows[0].shape[2]
    for f in range(4):

        @pl.when(lax.axis_index("fsdp") == f)
        def _(f=f):
            out = None
            for k, w in blocks.items():
                z = f ^ k
                for i, core in enumerate(cores):
                    y = jnp.dot(
                        rows[2 * i + z // 2][z % 2],
                        w[core * depth : (core + 1) * depth, :],
                        preferred_element_type=jnp.float32,
                    )
                    out = y if out is None else out + y
            put(out)


def own_products(own, near, far, low, high, total):
    def put(x):
        total[...] = x

    add_products((low, high), {0: own, 1: near, 2: far}, (0,), put)


def other_products(own, near, far, low, high, before, total):
    def put(x):
        total[...] = before[...] + x

    add_products((low, high), {0: own, 1: near, 2: far}, (1,), put)


def last_product(last, *refs):
    rows, (total, mine, one, two, other, held) = refs[:4], refs[4:]
    g, n = lax.axis_index("grp"), mine.shape[0]

    def put(x):
        held[...] = total[...] + x

    add_products(rows, {3: last}, (0, 1), put)
    for k, out in enumerate((mine, one, two, other)):
        at = pl.multiple_of(jnp.maximum((g ^ k) - 1, 0) * n, n)
        out[...] = held[pl.ds(at, n), :].astype(out.dtype)


def blank(after, out, token, held, sem):
    del after
    token[...] = jnp.zeros_like(token)

    @pl.when(lax.axis_index("grp") == 0)
    def _():
        held[...] = jnp.zeros_like(held)
        copy = pltpu.make_async_copy(held, out, sem)
        copy.start()
        copy.wait()


def attention(counts, mine, one, two, three, q_ref, blank_ref, out_ref, held, sems):
    del blank_ref
    g = lax.axis_index("grp")
    groups_q = QH // KVH
    copies = [
        pltpu.make_async_copy(held.at[at, :], out_ref.at[at, :], sems.at[s])
        for s, at in enumerate(pl.ds(s * TXT_S, TXT_S) for s in range(SAMP))
    ]

    @pl.when(g > 0)
    def _():
        kv = mine[...]
        for part in (one, two, three):
            kv = kv + part[...].astype(jnp.float32)
        kv = kv.astype(jnp.bfloat16)
        slot = lax.broadcasted_iota(jnp.int32, (CAP, 1), 0)
        width = 2 * HD
        pairs = [(s, k) for s in range(SAMP) for k in range(kv.shape[1] // width)]
        block = {
            (s, k): kv[s * CAP : s * CAP + CAP, k * width : (k + 1) * width] for s, k in pairs
        }
        rows = [slice(s * TXT_S, s * TXT_S + TXT_S) for s in range(SAMP)]

        def heads(k):
            return [slice(h * HD, (h + 1) * HD) for h in range(k * groups_q, (k + 1) * groups_q)]

        scores = {}
        for s, k in pairs:
            query = jnp.concatenate([q_ref[rows[s], h] for h in heads(k)], axis=0)
            scores[s, k] = lax.dot_general(
                block[s, k][:, :HD],
                query,
                (((1,), (1,)), ((), ())),
                preferred_element_type=jnp.float32,
            ) * (1.0 / HD**0.5)
        for s, copy in enumerate(copies):
            live = slot < counts[s : s + 1, :1]
            weights = {}
            for k in [k for r, k in pairs if r == s]:
                x = jnp.where(live, scores[s, k], -1e30)
                expo = jnp.exp(x - jnp.max(x, axis=0, keepdims=True))
                weights[k] = (expo / jnp.sum(expo, axis=0, keepdims=True)).astype(jnp.bfloat16)
            for k, w in weights.items():
                out = lax.dot_general(
                    w,
                    block[s, k][:, HD:],
                    (((0,), (0,)), ((), ())),
                    preferred_element_type=jnp.float32,
                )
                for j, h in enumerate(heads(k)):
                    held[rows[s], h] = out[j * TXT_S : (j + 1) * TXT_S].astype(jnp.bfloat16)
            copy.start()
        for copy in copies:
            copy.wait()


def shards_line(image_rows, enc_gain, key_value_w, tiles, queries):
    g, t = lax.axis_index("grp"), lax.axis_index("tp")
    n_rows = image_rows.shape[0]
    per_group = n_rows // 3
    half = key_value_w.shape[1] // 2
    quarter = key_value_w.shape[0] // 4
    bf16, f32 = jnp.bfloat16, jnp.float32
    planes = range(4)

    def send(x, pairs):
        index = lambda p, c: (p[0] * 4 + p[1]) * 2 + c
        return lax.ppermute(x, AXES, [(index(a, c), index(b, c)) for a, b in pairs for c in (0, 1)])

    def swap(x):
        return lax.ppermute(x, "tp", [(0, 1), (1, 0)])

    w = lax.dynamic_slice_in_dim(key_value_w, g * quarter, quarter, axis=0)
    kept = lax.dynamic_slice_in_dim(w, t * half, half, axis=1)
    given = lax.dynamic_slice_in_dim(w, (1 - t) * half, half, axis=1)
    shape = (2 * quarter, half)
    other = swap(given)
    own = call(join, [(shape, bf16)], kept, other, cost=1)[0]

    def swap_planes(x, k):
        return send(x, [((c, z), (c, z ^ k)) for c in range(4) for z in planes])

    near, far = swap_planes(own, 1), swap_planes(kept, 2)
    far = call(later, [(kept.shape, bf16)], far, kept, specs=[VMEM, ANY], cost=EARLY)[0]

    squares = call(row_squares, [((n_rows, 128), f32)], image_rows, own, specs=[VMEM, ANY])[0]
    whole, part = ((4, n_rows, quarter), bf16), ((2, n_rows, quarter), bf16)
    a, b, c, d_low, d_high = call(
        normalise,
        [whole] * 3 + [part] * 2,
        image_rows,
        squares,
        swap(squares),
        enc_gain.reshape(-1, 128),
    )
    other_far = call(later, [(kept.shape, bf16)], other, a, specs=[VMEM, ANY], cost=0)[0]
    other_far = swap_planes(other_far, 2)
    to_b, to_c, to_d = ([((0, z), (h, z)) for z in planes] for h in (1, 2, 3))
    d_high, b = send(d_high, to_c), send(b, to_b)
    c = call(later, [whole], c, far, specs=[VMEM, ANY], cost=0)[0]
    d_low = call(later, [part], d_low, b, specs=[VMEM, ANY], cost=0)[0]
    c, d_low = send(c, to_c), send(d_low, to_d)
    zeros, token = call(
        blank,
        [(queries.shape, bf16), ((8, 128), f32)],
        d_high,
        out_spec=[ANY, VMEM],
        specs=[ANY],
        cost=0,
        scratch=[pltpu.VMEM(queries.shape, bf16), pltpu.SemaphoreType.DMA],
    )
    specs = [VMEM, VMEM, ANY, ANY]
    far = call(join_later, [(shape, bf16)], far, other_far, near, token, specs=specs, cost=COST)[0]
    last = swap_planes(far, 1)
    d_high = send(d_high, [((2, z), (3, z)) for z in planes])
    rows = call(landed, [part] * 2, a, b, c, d_low, d_high)
    others = [swap(x) for x in rows]

    total, blocks = [((n_rows, half), f32)], (own, near, far)
    before = call(own_products, total, *blocks, *rows, cost=0)[0]
    total = call(other_products, total, *blocks, *others, before, cost=0)[0]
    counts = lax.dynamic_slice_in_dim(tiles, jnp.maximum(g - 1, 0) * SAMP, SAMP) * TILE_TOK
    message = (per_group, half)
    mine, *parts = call(
        last_product,
        [(message, f32)] + [(message, bf16)] * 3,
        last,
        *rows,
        *others,
        total,
        scratch=[pltpu.VMEM((n_rows, half), f32)],
    )
    parts = [
        send(x, [((c, z), (c ^ k, z)) for c in range(4) for z in planes])
        for k, x in zip((3, 2, 1), (parts[2], parts[1], parts[0]))
    ]
    return call(
        attention,
        [(queries.shape, bf16)],
        jnp.broadcast_to(counts[:, None], (SAMP, 128)),
        mine,
        *parts,
        queries,
        zeros,
        specs=[VMEM] * 6 + [ANY],
        out_spec=ANY,
        aliases={6: 0},
        scratch=[pltpu.VMEM(queries.shape, bf16), pltpu.SemaphoreType.DMA((SAMP,))],
    )[0]


def solution(mesh):
    sizes = tuple(mesh.shape[a] for a in AXES)
    return jax.shard_map(
        shards_line if sizes == (4, 4, 2) else shards_any,
        mesh=mesh,
        in_specs=(
            P(("grp", "fsdp"), "tp"),
            P("tp"),
            P(("tp", "fsdp"), None),
            P("fsdp"),
            P(("grp", "fsdp"), "tp"),
        ),
        out_specs=P(("grp", "fsdp"), "tp"),
        check_vma=False,
    )
```
